256 devices in a mesh: lat: 32 (over z, x), lon: 2 (over core), frame: 4 (over y).
Axes of the slice: x: 4, y: 4, z: 8, core: 2. Of those that a mesh axis runs over, the one named last changes fastest.
Arguments:
- frames_in: bfloat16 [4, 512, 32, 1024], P('frame', 'lat', 'lon'), may hold values from -64 to 64
- w_query: bfloat16 [1024, 1024], replicated
- w_key: bfloat16 [1024, 1024], replicated
- w_value: bfloat16 [1024, 1024], replicated, may hold values from -0.1875 to 0.1875
- w_out: bfloat16 [1024, 1024], replicated, may hold values from -0.1875 to 0.1875
- codes: int32 [4, 64, 4, 9], P('frame', 'lat', 'lon'), may hold values from 0 to 8, as said below
- counts: int32 [4, 64, 4], P('frame', 'lat', 'lon'), may hold values from 3 to 9, as said below
Outputs:
- output: bfloat16 [4, 512, 32, 1024], P('frame', 'lat', 'lon')
The draws below stay inside these ranges and needn't reach their ends.
Inputs may be any that keep to these rules, and one draw needn't show every extreme that they name: codes[f, r, c] holds each of the nine window positions 0 to 8 once; position code means window row code // 3 and window column code % 3. counts is 6 to 9 in the first and the last 16 tile rows and 3 to 6 in the others.
All inputs are finite; a program needn't handle non-finite values.
Results may differ from the reference program's by a relative error of at most 0.008.
Values may be sent and summed in bfloat16 or wider, within the bound.
A program may use at most 192 MiB of HBM per device.

```python
import math
import jax
import jax.numpy as jnp
from jax import lax

D = 1024
HEADS = 16
HEAD = 64
TILE = 8
WIN = 9
FRAMES = 4
NTLAT = 64
NTLON = 4
NLAT = 512
NLON = 32


def draw_frames_in(key, part):
    array_shape = (FRAMES, NLAT, NLON, D)
    values = jnp.clip(jax.random.normal(key, array_shape, jnp.float32), -6.0, 6.0)
    return values.astype(jnp.bfloat16)


def pair_weights(key):
    first = jnp.clip(jax.random.normal(jax.random.fold_in(key, 11), (D, D), jnp.float32), -6.0, 6.0)
    second = jnp.clip(jax.random.normal(jax.random.fold_in(key, 12), (D, D), jnp.float32), -6.0, 6.0)
    return (first, second)


def draw_w_query(key, part):
    first, second = pair_weights(key)
    return (first * D ** (-0.5)).astype(jnp.bfloat16)


def draw_w_key(key, part):
    first, second = pair_weights(key)
    mixed_draw = second
    return (mixed_draw * D ** (-0.5)).astype(jnp.bfloat16)


def draw_codes(key, part):
    raw_scores = jax.random.randint(key, (FRAMES, NTLAT, NTLON, WIN), 0, 2 ** 20) * 16
    raw_scores = raw_scores + jnp.arange(WIN, dtype=jnp.int32)
    return jnp.argsort(raw_scores, axis=-1, stable=True).astype(jnp.int32)


def draw_counts(key, part):
    base_count = jax.random.randint(key, (FRAMES, NTLAT, NTLON), 3, 7)
    tile_rows = jnp.arange(NTLAT, dtype=jnp.int32)[None, :, None]
    edge_rows = NTLAT // 4
    polar = jnp.logical_or(tile_rows < edge_rows, tile_rows >= NTLAT - edge_rows)
    return (base_count + 3 * polar.astype(jnp.int32)).astype(jnp.int32)


def centred(rng, dims, width, bound, kind=jnp.bfloat16):
    drawn = jax.random.normal(rng, dims, jnp.float32) * width
    return jnp.minimum(jnp.maximum(drawn, -bound), bound).astype(kind)


def setup_inputs(seed: int = 0) -> dict:
    key_of = jax.random.split(jax.random.key(seed), 8)
    frames_in = draw_frames_in(jax.random.fold_in(key_of[7], 71), 0)
    w_query = draw_w_query(jax.random.fold_in(key_of[7], 71), 0)
    w_key = draw_w_key(jax.random.fold_in(key_of[7], 71), 0)
    w_value = centred(key_of[3], (D, D), D ** -0.5, 0.1875)
    w_out = centred(key_of[4], (D, D), D ** -0.5, 0.1875)
    codes = draw_codes(jax.random.fold_in(key_of[7], 71), 0)
    counts = draw_counts(jax.random.fold_in(key_of[7], 71), 0)
    return {"frames_in": frames_in, "w_query": w_query, "w_key": w_key, "w_value": w_value, "w_out": w_out, "codes": codes, "counts": counts}


def tiles_of(array, last):
    shaped = array.reshape(FRAMES, NTLAT, TILE, NTLON, TILE, last)
    return shaped.transpose(0, 1, 3, 2, 4, 5).reshape(FRAMES * NTLAT * NTLON, TILE * TILE, last)

def reference(frames_in, w_query, w_key, w_value, w_out, codes, counts):
    flat_cells = frames_in.reshape(-1, D)
    queries = jnp.dot(flat_cells, w_query, preferred_element_type=jnp.float32).astype(jnp.bfloat16)
    key_all = jnp.dot(flat_cells, w_key, preferred_element_type=jnp.float32).astype(jnp.bfloat16)
    value_all = jnp.dot(flat_cells, w_value, preferred_element_type=jnp.float32).astype(jnp.bfloat16)
    pair_tiles = tiles_of(jnp.concatenate([key_all, value_all], axis=-1), 2 * D)
    query_tiles = tiles_of(queries, D).reshape(FRAMES * NTLAT, NTLON, TILE * TILE, HEADS, HEAD)
    code_rows = codes.reshape(FRAMES * NTLAT, NTLON, WIN)
    count_rows = counts.reshape(FRAMES * NTLAT, NTLON)
    score_scale = 1.0 / math.sqrt(HEAD)

    def one_row(operands):
        row_id, row_q, row_codes, row_counts = operands
        frame_id = row_id // NTLAT
        tile_row = row_id % NTLAT
        start_row = jnp.clip(tile_row - 1, 0, NTLAT - 3)
        rows_hit = start_row + row_codes // 3
        cols_hit = (jnp.arange(NTLON, dtype=jnp.int32)[:, None] + row_codes % 3 - 1) % NTLON
        own_index = (frame_id * NTLAT + rows_hit) * NTLON + cols_hit
        earlier_index = (jnp.maximum(frame_id - 1, 0) * NTLAT + rows_hit) * NTLON + cols_hit
        both_index = jnp.stack([own_index, earlier_index]).reshape(-1).astype(jnp.int32)
        chosen = jnp.take(pair_tiles, both_index, axis=0).reshape(2, NTLON, WIN, TILE * TILE, 2 * D).astype(jnp.float32)
        key_part = chosen[..., :D].reshape(2, NTLON, WIN, TILE * TILE, HEADS, HEAD)
        value_part = chosen[..., D:].reshape(2, NTLON, WIN, TILE * TILE, HEADS, HEAD)
        scores = jnp.einsum('gqhd,sgjkhd->ghqsjk', row_q.astype(jnp.float32), key_part) * score_scale
        live_slots = jnp.arange(WIN, dtype=jnp.int32)[None, :] < row_counts[:, None]
        live_both = jnp.stack([live_slots, jnp.logical_and(live_slots, frame_id > 0)], axis=1)
        allowed = live_both[:, None, None, :, :, None]
        scores = jnp.where(allowed, scores, -1e+30)
        row_max = lax.optimization_barrier(jnp.max(scores, axis=(3, 4, 5), keepdims=True))
        exponent = jnp.exp(scores - row_max)
        denominator = lax.optimization_barrier(jnp.sum(exponent, axis=(3, 4, 5)))
        weights = lax.optimization_barrier(exponent.astype(jnp.bfloat16)).astype(jnp.float32)
        combined = jnp.einsum('ghqsjk,sgjkhd->gqhd', weights, value_part)
        combined = combined / jnp.transpose(denominator, (0, 2, 1))[..., None]
        return combined.astype(jnp.bfloat16).reshape(NTLON, TILE * TILE, D)
    row_ids = jnp.arange(FRAMES * NTLAT, dtype=jnp.int32)
    attended = lax.map(one_row, (row_ids, query_tiles, code_rows, count_rows))
    attended = attended.reshape(FRAMES, NTLAT, NTLON, TILE, TILE, D).transpose(0, 1, 3, 2, 4, 5).reshape(-1, D)
    output = jnp.dot(attended, w_out, preferred_element_type=jnp.float32).astype(jnp.bfloat16)
    return output.reshape(FRAMES, NLAT, NLON, D)
```

```python
import functools

import jax
import jax.numpy as jnp
from jax import lax
from jax.experimental import pallas as pl
from jax.experimental.pallas import tpu as pltpu
from jax.sharding import PartitionSpec as P

HEADS = 16
HEAD = 64
TILE = 8
WIN = 9
D = 1024
HALF = D // 2
TOK = 128
NC = 4
CH = TOK // NC
VROWS = HEAD + 16
DEAD = -1e38
FLOOR = -1e30
MESH = pl.DeviceIdType.MESH
COMM = True
NT = (((1,), (1,)), ((), ()))
TN = (((0,), (0,)), ((), ()))


def kernel(
    x_ref, wq_ref, wk_ref, wv_ref, wo_ref, codes_ref, counts_ref, out_ref,
    xs, wq, wk, wv, wo, wvt, qz, ks, vt, os_, ms, bias, snd, full,
    w_sem, x_sem,
    p_ss, p_rs, y_ss, y_rs, n0_ss, n0_rs, n1_ss, n1_rs, f_ss, f_rs, b_ss, b_rs, a_ss, a_rs,
):
    f32, bf16 = jnp.float32, jnp.bfloat16
    lat, c, frame = lax.axis_index("lat"), lax.axis_index("lon"), lax.axis_index("frame")
    nlat, nframe = lax.axis_size("lat"), lax.axis_size("frame")
    o = 1 - c
    has_n, has_s = lat > 0, lat < nlat - 1
    has_prev, has_next = frame > 0, frame < nframe - 1

    cols = pl.ds(pl.multiple_of(c * HALF, HALF), HALF)
    x_copies = [pltpu.make_async_copy(x_ref.at[r], xs.at[0, 1 + r, c], x_sem.at[r]) for r in range(2)]
    w_copies = [
        pltpu.make_async_copy(wv_ref.at[:, cols], wv, w_sem.at[0]),
        pltpu.make_async_copy(wk_ref.at[:, cols], wk, w_sem.at[1]),
        pltpu.make_async_copy(wq_ref.at[:, cols], wq, w_sem.at[2]),
        pltpu.make_async_copy(wo_ref, wo, w_sem.at[3]),
    ]
    for copy in x_copies:
        copy.start()
    for copy in w_copies:
        copy.start()

    def remote(src, dst, ss, rs, dev):
        return pltpu.make_async_remote_copy(
            src_ref=src, dst_ref=dst, send_sem=ss, recv_sem=rs, device_id=dev, device_id_type=MESH
        )

    def part(i):
        return pl.ds(pl.multiple_of(i * CH, CH), CH)

    def own_to_peer(r, lon):
        return remote(x_ref.at[r], xs.at[0, 1 + r, lon], p_ss.at[r], p_rs.at[r], {"lon": o})

    def to_next(r, i):
        k = r * NC + i
        return remote(x_ref.at[r, part(i)], xs.at[1, 1 + r, c, part(i)], y_ss.at[k], y_rs.at[k], {"frame": frame + 1})

    def side_dev(side):
        return {"lat": lat - 1 if side == 0 else lat + 1}

    def own_to_side(side, i):
        k = side * NC + i
        return remote(
            x_ref.at[side, part(i)], xs.at[0, 3 - 3 * side, c, part(i)], n0_ss.at[k], n0_rs.at[k], side_dev(side)
        )

    def prev_to_side(side, i):
        k = side * NC + i
        return remote(
            xs.at[1, 1 + side, c, part(i)], xs.at[1, 3 - 3 * side, c, part(i)], n1_ss.at[k], n1_rs.at[k], side_dev(side)
        )

    def forward(fr, row, i, lon):
        k = (fr * 4 + row) * NC + i
        block = xs.at[fr, row, lon, part(i)]
        return remote(block, block, f_ss.at[k], f_rs.at[k], {"lon": o})

    def bias_to_peer(lon):
        return remote(bias.at[lon], bias.at[lon], b_ss.at[0], b_rs.at[0], {"lon": o})

    def att_to_peer(r, lon):
        return remote(snd.at[r], full.at[r, lon], a_ss.at[r], a_rs.at[r], {"lon": o})

    send_to = (has_n, has_s)
    gets_from = (has_s, has_n)

    if COMM:
        barrier = pltpu.get_barrier_semaphore()

        def greet(dev):
            pl.semaphore_signal(barrier, inc=1, device_id=dev, device_id_type=MESH)

        greet({"lon": o})
        pl.when(has_n)(lambda: greet({"lat": lat - 1}))
        pl.when(has_s)(lambda: greet({"lat": lat + 1}))
        pl.when(has_prev)(lambda: greet({"frame": frame - 1}))
        pl.when(has_next)(lambda: greet({"frame": frame + 1}))

    ri = lax.broadcasted_iota(jnp.int32, (8, TOK), 0)
    li = lax.broadcasted_iota(jnp.int32, (8, TOK), 1)
    second = (li // TILE) % 2 == 1
    gcol = 2 * c + (li // TILE) % 2
    wcol = (ri - gcol + 5) % 4
    first_ext = []
    outer = [jnp.where(has_n, 0, 3), jnp.where(has_s, 3, 0)]
    for r in range(2):
        first = jnp.minimum(jnp.maximum(2 * lat + r - 1, 0), 2 * nlat - 3) - 2 * lat + 1
        first_ext.append(first)
        cnt = jnp.where(second, counts_ref[0, r, 1], counts_ref[0, r, 0])
        for slot in range(3):
            ext = outer[r] if slot == 0 else slot
            want = jnp.where(jnp.logical_and(wcol < 3, ri < 4), 3 * (ext - first) + wcol, -1)
            live = jnp.zeros((8, TOK), f32)
            for j in range(WIN):
                code = jnp.where(second, codes_ref[0, r, 1, j], codes_ref[0, r, 0, j])
                hit = jnp.logical_and(code == want, j < cnt)
                live = jnp.where(hit, 1.0, live)
            bias[c, r, slot] = jnp.where(live > 0.5, 0.0, DEAD)
    vt[:, :, :, HEAD:, :] = jnp.ones((2, 4, 8, VROWS - HEAD, 2 * TOK), bf16)

    if COMM:
        greeted = (
            1
            + has_n.astype(jnp.int32)
            + has_s.astype(jnp.int32)
            + has_prev.astype(jnp.int32)
            + has_next.astype(jnp.int32)
        )
        pl.semaphore_wait(barrier, greeted)
        for r in range(2):
            own_to_peer(r, c).start()

        @pl.when(has_next)
        def _():
            for i in range(NC):
                to_next(0, i).start()

        for side in range(2):

            @pl.when(send_to[side])
            def _(side=side):
                for i in range(NC):
                    own_to_side(side, i).start()

        @pl.when(has_next)
        def _():
            for i in range(NC):
                to_next(1, i).start()

        bias_to_peer(c).start()

    def pump_own_sides(i):
        for side in range(2):

            @pl.when(gets_from[side])
            def _(side=side):
                own_to_side(side, i).wait_recv()
                forward(0, 3 - 3 * side, i, c).start()

    def pump_prev(r, i):
        @pl.when(has_prev)
        def _():
            to_next(r, i).wait_recv()

            @pl.when(send_to[r])
            def _():
                prev_to_side(r, i).start()

            forward(1, 1 + r, i, c).start()

    def pump_prev_side(side, i):
        @pl.when(jnp.logical_and(has_prev, gets_from[side]))
        def _():
            prev_to_side(side, i).wait_recv()
            forward(1, 3 - 3 * side, i, c).start()

    def project(fr, row):
        x = xs[fr, row].reshape(2 * TOK, D)
        key = jnp.dot(x, wk[...], preferred_element_type=f32).astype(bf16)
        for pair in range(4):
            ks[fr, row, pair] = key[:, pair * 128 : (pair + 1) * 128]
        value = lax.dot_general(wvt[...], x, NT, preferred_element_type=f32).astype(bf16)
        vt[fr, row, :, :HEAD, :] = value.reshape(8, HEAD, 2 * TOK)

    def attend(fr, rows_slots, r, pair, first):
        for j in range(2):
            h = 2 * pair + j
            q = qz[r, h]
            parts = []
            best = None
            for row, slot in rows_slots:
                s = lax.dot_general(ks[fr, row, pair], q, NT, preferred_element_type=f32)
                s = s.reshape(2, TILE, 2, TILE, 2 * TOK)
                b = jnp.concatenate([bias[0, r, slot], bias[1, r, slot]], axis=1)[:4]
                b = b.reshape(2, 2, 1, 2 * TOK)
                top = jnp.max(s, axis=1) + b
                top = jnp.max(jnp.max(top, axis=0), axis=0)
                best = top if best is None else jnp.maximum(best, top)
                parts.append((s, b, row))
            m = jnp.maximum(jnp.max(best, axis=0, keepdims=True), FLOOR)
            if not first:
                m_old = ms[r, h, :1]
                m = jnp.maximum(m, m_old)
            total = None
            for s, b, row in parts:
                p = jnp.exp(s + (b - m)[:, None]).reshape(2 * TOK, 2 * TOK).astype(bf16)
                t = jnp.dot(vt[fr, row, h], p, preferred_element_type=f32)
                total = t if total is None else total + t
            if not first:
                total = total + os_[r, h] * jnp.exp(m_old - m)
            os_[r, h] = total
            ms[r, h] = jnp.broadcast_to(m, (8, 2 * TOK))

    w_copies[0].wait()
    wvt[...] = wv[...].T
    for copy in x_copies:
        copy.wait()
    if COMM:
        for r in range(2):
            own_to_peer(r, o).wait_recv()
        bias_to_peer(o).wait_recv()
    w_copies[1].wait()
    w_copies[2].wait()
    low = lax.broadcasted_iota(jnp.int32, (2 * TOK, 128), 1) < HEAD

    @pl.loop(0, 2)
    def _(r):
        project(0, 1 + r)
        x = xs[0, 1 + r].reshape(2 * TOK, D)
        query = jnp.dot(x, wq[...], preferred_element_type=f32).astype(bf16).astype(f32) * 0.125
        for pair in range(4):
            q = query[:, pair * 128 : (pair + 1) * 128]
            qz[r, 2 * pair] = jnp.where(low, q, 0.0).astype(bf16)
            qz[r, 2 * pair + 1] = jnp.where(low, 0.0, q).astype(bf16)

    @pl.loop(0, 4)
    def _(g):
        for u in range(2):
            attend(0, [(1, 1), (2, 2)], g // 2, (g % 2) * 2 + u, True)
        if COMM:
            pump_own_sides(g)
            pump_prev(0, g)

    for side in range(2):

        @pl.when(gets_from[side])
        def _(side=side):
            if COMM:
                for i in range(NC):
                    forward(0, 3 - 3 * side, i, o).wait_recv()
            project(0, 3 - 3 * side)

    @pl.loop(0, 4)
    def _(g):
        r = g // 2
        row = jnp.where(r == 0, outer[0], outer[1])
        for u in range(2):
            attend(0, [(row, 0)], r, (g % 2) * 2 + u, False)
        if COMM:
            pump_prev(1, g)

    @pl.when(has_prev)
    def _():
        @pl.loop(0, 2)
        def _(r0):
            row = 1 + r0
            if COMM:
                for i in range(NC):
                    forward(1, row, i, o).wait_recv()
            project(1, row)

            @pl.loop(0, 8)
            def _(g):
                attend(1, [(row, row)], g // 4, g % 4, False)

        for side in range(2):

            @pl.when(gets_from[side])
            def _(side=side):
                if COMM:
                    for i in range(NC):
                        pump_prev_side(side, i)
                    for i in range(NC):
                        forward(1, 3 - 3 * side, i, o).wait_recv()
                project(1, 3 - 3 * side)

        @pl.loop(0, 8)
        def _(g):
            r = g // 4
            row = jnp.where(r == 0, outer[0], outer[1])
            attend(1, [(row, 0)], r, g % 4, False)

    w_copies[3].wait()
    for r in range(2):
        for h in range(8):
            total = os_[r, h]
            att = (total[:HEAD] * (1.0 / total[HEAD : HEAD + 1])).astype(bf16)
            rows = pl.ds(h * HEAD, HEAD)
            mine_first = c == 0
            full[r, c, rows] = jnp.where(mine_first, att[:, :TOK], att[:, TOK:])
            snd[r, rows] = jnp.where(mine_first, att[:, TOK:], att[:, :TOK])
        if COMM:
            att_to_peer(r, c).start()
    for r in range(2):
        if COMM:
            att_to_peer(r, o).wait_recv()
        a = full[r].reshape(D, TOK)
        out_ref[r] = lax.dot_general(a, wo[...], TN, preferred_element_type=f32).astype(bf16)

    if COMM:
        for r in range(2):
            own_to_peer(r, c).wait_send()
            att_to_peer(r, c).wait_send()
        bias_to_peer(c).wait_send()

        @pl.when(has_next)
        def _():
            for r in range(2):
                for i in range(NC):
                    to_next(r, i).wait_send()

        for side in range(2):

            @pl.when(send_to[side])
            def _(side=side):
                for i in range(NC):
                    own_to_side(side, i).wait_send()

            @pl.when(gets_from[side])
            def _(side=side):
                for i in range(NC):
                    forward(0, 3 - 3 * side, i, c).wait_send()

        @pl.when(has_prev)
        def _():
            for side in range(2):
                for i in range(NC):
                    forward(1, 1 + side, i, c).wait_send()

                @pl.when(send_to[side])
                def _(side=side):
                    for i in range(NC):
                        prev_to_side(side, i).wait_send()

                @pl.when(gets_from[side])
                def _(side=side):
                    for i in range(NC):
                        forward(1, 3 - 3 * side, i, c).wait_send()


def on_device(frames_in, w_query, w_key, w_value, w_out, codes, counts):
    shape = frames_in.shape
    x = frames_in.reshape(2, TOK, D)
    bf16, f32 = jnp.bfloat16, jnp.float32
    dma = pltpu.SemaphoreType.DMA
    anywhere = pl.BlockSpec(memory_space=pl.ANY)
    scalars = pl.BlockSpec(memory_space=pltpu.SMEM)
    out = pl.pallas_call(
        kernel,
        out_shape=jax.ShapeDtypeStruct((2, TOK, D), bf16),
        in_specs=[anywhere] * 5 + [scalars] * 2,
        out_specs=pl.BlockSpec(memory_space=pltpu.VMEM),
        scratch_shapes=[
            pltpu.VMEM((2, 4, 2, TOK, D), bf16),
            pltpu.VMEM((D, HALF), bf16),
            pltpu.VMEM((D, HALF), bf16),
            pltpu.VMEM((D, HALF), bf16),
            pltpu.VMEM((D, D), bf16),
            pltpu.VMEM((HALF, D), bf16),
            pltpu.VMEM((2, 8, 2 * TOK, 128), bf16),
            pltpu.VMEM((2, 4, 4, 2 * TOK, 128), bf16),
            pltpu.VMEM((2, 4, 8, VROWS, 2 * TOK), bf16),
            pltpu.VMEM((2, 8, VROWS, 2 * TOK), f32),
            pltpu.VMEM((2, 8, 8, 2 * TOK), f32),
            pltpu.VMEM((2, 2, 3, 8, TOK), f32),
            pltpu.VMEM((2, HALF, TOK), bf16),
            pltpu.VMEM((2, 2, HALF, TOK), bf16),
            dma((4,)),
            dma((2,)),
            dma((2,)),
            dma((2,)),
            dma((2 * NC,)),
            dma((2 * NC,)),
            dma((2 * NC,)),
            dma((2 * NC,)),
            dma((2 * NC,)),
            dma((2 * NC,)),
            dma((8 * NC,)),
            dma((8 * NC,)),
            dma((1,)),
            dma((1,)),
            dma((2,)),
            dma((2,)),
        ],
        compiler_params=pltpu.CompilerParams(
            vmem_limit_bytes=50 << 20,
            **(dict(collective_id=0, has_side_effects=True) if COMM else {}),
        ),
        cost_estimate=pl.CostEstimate(flops=12 * 10**9, bytes_accessed=8 << 20, transcendentals=6 << 20),
    )(x, w_query, w_key, w_value, w_out, codes, counts)
    return out.reshape(shape)


def solution(mesh):
    placed = (
        P("frame", "lat", "lon", None),
        P(),
        P(),
        P(),
        P(),
        P("frame", "lat", "lon", None),
        P("frame", "lat", "lon"),
    )
    return jax.shard_map(
        on_device,
        mesh=mesh,
        in_specs=placed,
        out_specs=P("frame", "lat", "lon", None),
        check_vma=False,
    )
```

```python
import functools

import jax
import jax.numpy as jnp
from jax import lax
from jax.experimental import pallas as pl
from jax.experimental.pallas import tpu as pltpu
from jax.sharding import PartitionSpec as P

HEADS = 16
HEAD = 64
TILE = 8
WIN = 9
D = 1024
HALF = D // 2
TOK = 128
NC = 4
CH = TOK // NC
VROWS = HEAD + 16
DEAD = -1e38
FLOOR = -1e30
MESH = pl.DeviceIdType.MESH
COMM = True
NT = (((1,), (1,)), ((), ()))
TN = (((0,), (0,)), ((), ()))


def kernel(
    x_ref, wq_ref, wk_ref, wv_ref, wo_ref, codes_ref, counts_ref, out_ref,
    xs, wq, wk, wv, wo, wvt, qz, ks, vt, os_, ms, bias, snd, full,
    s0, s1, s2, s3, s4, s5, s6, s7,
    w_sem, x_sem,
    p_ss, p_rs, y_ss, y_rs, n0_ss, n0_rs, n1_ss, n1_rs, f_ss, f_rs, b_ss, b_rs, a_ss, a_rs,
):
    f32, bf16 = jnp.float32, jnp.bfloat16
    lat, c, frame = lax.axis_index("lat"), lax.axis_index("lon"), lax.axis_index("frame")
    nlat, nframe = lax.axis_size("lat"), lax.axis_size("frame")
    o = 1 - c
    ss = (s0, s1, s2, s3, s4, s5, s6, s7)
    has_n, has_s = lat > 0, lat < nlat - 1
    has_prev, has_next = frame > 0, frame < nframe - 1

    cols = pl.ds(pl.multiple_of(c * HALF, HALF), HALF)
    x_copies = [pltpu.make_async_copy(x_ref.at[r], xs.at[0, 1 + r, c], x_sem.at[r]) for r in range(2)]
    w_copies = [
        pltpu.make_async_copy(wv_ref.at[:, cols], wv, w_sem.at[0]),
        pltpu.make_async_copy(wk_ref.at[:, cols], wk, w_sem.at[1]),
        pltpu.make_async_copy(wq_ref.at[:, cols], wq, w_sem.at[2]),
        pltpu.make_async_copy(wo_ref, wo, w_sem.at[3]),
    ]
    for copy in x_copies:
        copy.start()
    for copy in w_copies:
        copy.start()

    def remote(src, dst, ss, rs, dev):
        return pltpu.make_async_remote_copy(
            src_ref=src, dst_ref=dst, send_sem=ss, recv_sem=rs, device_id=dev, device_id_type=MESH
        )

    def part(i):
        return pl.ds(pl.multiple_of(i * CH, CH), CH)

    def own_to_peer(r, lon):
        return remote(x_ref.at[r], xs.at[0, 1 + r, lon], p_ss.at[r], p_rs.at[r], {"lon": o})

    def to_next(r, i):
        k = r * NC + i
        return remote(x_ref.at[r, part(i)], xs.at[1, 1 + r, c, part(i)], y_ss.at[k], y_rs.at[k], {"frame": frame + 1})

    def side_dev(side):
        return {"lat": lat - 1 + 2 * side}

    def own_to_side(side, i):
        k = side * NC + i
        return remote(
            x_ref.at[side, part(i)], xs.at[0, 3 - 3 * side, c, part(i)], n0_ss.at[k], n0_rs.at[k], side_dev(side)
        )

    def prev_to_side(side, i):
        k = side * NC + i
        return remote(
            xs.at[1, 1 + side, c, part(i)], xs.at[1, 3 - 3 * side, c, part(i)], n1_ss.at[k], n1_rs.at[k], side_dev(side)
        )

    def forward(fr, row, i, lon):
        k = (fr * 4 + row) * NC + i
        block = xs.at[fr, row, lon, part(i)]
        return remote(block, block, f_ss.at[k], f_rs.at[k], {"lon": o})

    def bias_to_peer(lon):
        return remote(bias.at[lon], bias.at[lon], b_ss.at[0], b_rs.at[0], {"lon": o})

    def att_to_peer(r, lon):
        return remote(snd.at[r], full.at[r, lon], a_ss.at[r], a_rs.at[r], {"lon": o})

    send_to = (has_n, has_s)
    gets_from = (has_s, has_n)

    if COMM:
        barrier = pltpu.get_barrier_semaphore()

        def greet(dev):
            pl.semaphore_signal(barrier, inc=1, device_id=dev, device_id_type=MESH)

        greet({"lon": o})
        pl.when(has_n)(lambda: greet({"lat": lat - 1}))
        pl.when(has_s)(lambda: greet({"lat": lat + 1}))
        pl.when(has_prev)(lambda: greet({"frame": frame - 1}))
        pl.when(has_next)(lambda: greet({"frame": frame + 1}))

    ri = lax.broadcasted_iota(jnp.int32, (8, TOK), 0)
    li = lax.broadcasted_iota(jnp.int32, (8, TOK), 1)
    second = (li // TILE) % 2 == 1
    gcol = 2 * c + (li // TILE) % 2
    wcol = (ri - gcol + 5) % 4
    first_ext = []
    outer = [jnp.where(has_n, 0, 3), jnp.where(has_s, 3, 0)]
    for r in range(2):
        first = jnp.minimum(jnp.maximum(2 * lat + r - 1, 0), 2 * nlat - 3) - 2 * lat + 1
        first_ext.append(first)
        cnt = jnp.where(second, counts_ref[0, r, 1], counts_ref[0, r, 0])
        for slot in range(3):
            ext = outer[r] if slot == 0 else slot
            want = jnp.where(jnp.logical_and(wcol < 3, ri < 4), 3 * (ext - first) + wcol, -1)
            live = jnp.zeros((8, TOK), f32)
            for j in range(WIN):
                code = jnp.where(second, codes_ref[0, r, 1, j], codes_ref[0, r, 0, j])
                hit = jnp.logical_and(code == want, j < cnt)
                live = jnp.where(hit, 1.0, live)
            bias[c, r, slot] = jnp.where(live > 0.5, 0.0, DEAD)
    vt[:, :, :, HEAD:, :] = jnp.ones((2, 4, 8, VROWS - HEAD, 2 * TOK), bf16)
    w_copies[0].wait()
    wvt[...] = wv[...].T

    if COMM:
        greeted = (
            1
            + has_n.astype(jnp.int32)
            + has_s.astype(jnp.int32)
            + has_prev.astype(jnp.int32)
            + has_next.astype(jnp.int32)
        )
        pl.semaphore_wait(barrier, greeted)
        for r in range(2):
            own_to_peer(r, c).start()

        @pl.when(has_next)
        def _():
            for i in range(NC):
                to_next(0, i).start()

        for side in range(2):

            @pl.when(send_to[side])
            def _(side=side):
                for i in range(NC):
                    own_to_side(side, i).start()

        @pl.when(has_next)
        def _():
            for i in range(NC):
                to_next(1, i).start()

        bias_to_peer(c).start()

    def pump_own_sides(i):
        for side in range(2):

            @pl.when(gets_from[side])
            def _(side=side):
                own_to_side(side, i).wait_recv()
                forward(0, 3 - 3 * side, i, c).start()

    def pump_prev(r, i):
        @pl.when(has_prev)
        def _():
            to_next(r, i).wait_recv()

            @pl.when(send_to[r])
            def _():
                prev_to_side(r, i).start()

            forward(1, 1 + r, i, c).start()

    def pump_prev_side(side, i):
        prev_to_side(side, i).wait_recv()
        forward(1, 3 - 3 * side, i, c).start()

    def project(x, fr, blk):
        key = jnp.dot(x, wk[...], preferred_element_type=f32).astype(bf16)
        for pair in range(4):
            ks[fr, blk, pair] = key[:, pair * 128 : (pair + 1) * 128]
        value = lax.dot_general(wvt[...], x, NT, preferred_element_type=f32).astype(bf16)
        vt[fr, blk, :, :HEAD, :] = value.reshape(8, HEAD, 2 * TOK)

    def row_of(fr, row):
        return xs[fr, row].reshape(2 * TOK, D)

    def attend(fr, blocks, r, first, group, ahead):
        n = len(blocks)
        masks = []
        for _, (a, b) in blocks:
            rows = [jnp.concatenate([bias[0, r, slot], bias[1, r, slot]], axis=1)[k : k + 2] for slot, k in (a, b)]
            masks.append([v.reshape(2, 1, 2 * TOK) for v in rows])

        def scores(h):
            best = None
            for k, (blk, _) in enumerate(blocks):
                s = lax.dot_general(ks[fr, blk, h // 2], qz[r, h], NT, preferred_element_type=f32)
                ss[(h * n + k) % 8][...] = s
                s = s.reshape(2, TILE, 2, TILE, 2 * TOK)
                for u in range(2):
                    top = jnp.max(jnp.max(s[u], axis=0) + masks[k][u], axis=0)
                    best = top if best is None else jnp.maximum(best, top)
            m = jnp.maximum(jnp.max(best, axis=0, keepdims=True), FLOOR)
            if first:
                return m, None
            m_old = ms[r, h, :1]
            return jnp.maximum(m, m_old), m_old

        def values(h, m, m_old):
            total = None
            for k, (blk, _) in enumerate(blocks):
                s = ss[(h * n + k) % 8][...].reshape(2, TILE, 2, TILE, 2 * TOK)
                p = [jnp.exp(s[u] + (masks[k][u] - m)[None]).reshape(TOK, 2 * TOK).astype(bf16) for u in range(2)]
                t = jnp.dot(vt[fr, blk, h], jnp.concatenate(p, axis=0), preferred_element_type=f32)
                total = t if total is None else total + t
            if not first:
                total = total + os_[r, h] * jnp.exp(m_old - m)
            os_[r, h] = total
            ms[r, h] = jnp.broadcast_to(m, (8, 2 * TOK))

        steps = 8 // group
        state = {}
        for g in range(steps + ahead):
            if g < steps:
                for h in range(g * group, (g + 1) * group):
                    state[h] = scores(h)
            if g >= ahead:
                for h in range((g - ahead) * group, (g - ahead + 1) * group):
                    values(h, *state.pop(h))

    low = lax.broadcasted_iota(jnp.int32, (TOK, 128), 1) < HEAD
    for copy in x_copies:
        copy.wait()
    w_copies[1].wait()
    w_copies[2].wait()

    @pl.loop(0, 2)
    def _(t):
        lon = jnp.where(t == 0, c, o)

        @pl.when(t == 1)
        def _():
            if COMM:
                for r in range(2):
                    own_to_peer(r, o).wait_recv()
                bias_to_peer(o).wait_recv()

        x = jnp.concatenate([xs[0, 1, lon], xs[0, 2, lon]], axis=0)
        project(x, 0, 1 + lon)
        query = jnp.dot(x, wq[...], preferred_element_type=f32).astype(bf16).astype(f32) * 0.125
        place = pl.ds(pl.multiple_of(lon * TOK, TOK), TOK)
        for r in range(2):
            for pair in range(4):
                q = query[r * TOK : (r + 1) * TOK, pair * 128 : (pair + 1) * 128]
                qz[r, 2 * pair, place] = jnp.where(low, q, 0.0).astype(bf16)
                qz[r, 2 * pair + 1, place] = jnp.where(low, 0.0, q).astype(bf16)

    @pl.loop(0, 2)
    def _(r):
        if COMM:
            for i in range(2):
                pump_own_sides(2 * r + i)
                pump_prev(0, 2 * r + i)
        attend(0, [(1, ((1, 0), (2, 0))), (2, ((1, 2), (2, 2)))], r, True, 2, 1)

    @pl.loop(0, 2)
    def _(side):
        @pl.when(jnp.where(side == 0, has_s, has_n))
        def _():
            row = 3 - 3 * side
            if COMM:
                for i in range(NC):
                    forward(0, row, i, o).wait_recv()
            project(row_of(0, row), 0, row)

    @pl.loop(0, 2)
    def _(r):
        if COMM:
            pump_prev(1, 2 * r)
            pump_prev(1, 2 * r + 1)
        row = jnp.where(r == 0, outer[0], outer[1])
        attend(0, [(row, ((0, 0), (0, 2)))], r, False, 4, 1)

    @pl.when(has_prev)
    def _():
        @pl.loop(0, 2)
        def _(t):
            row = 1 + t
            if COMM:
                for i in range(NC):
                    forward(1, row, i, o).wait_recv()
            project(row_of(1, row), 1, row)

            @pl.loop(0, 2)
            def _(r):
                attend(1, [(row, ((row, 0), (row, 2)))], r, False, 4, 1)

    mine_first = c == 0

    @pl.loop(0, 2)
    def _(t):
        r = 1 - t

        @pl.when(has_prev)
        def _():
            row = jnp.where(jnp.logical_and(t == 0, has_s), 3, 0)

            @pl.when(jnp.logical_or(t == 0, jnp.logical_and(has_n, has_s)))
            def _():
                if COMM:
                    side = jnp.where(row == 3, 0, 1)
                    for i in range(NC):
                        pump_prev_side(side, i)
                    for i in range(NC):
                        forward(1, row, i, o).wait_recv()
                project(row_of(1, row), 1, row)

            mask_row = jnp.where(r == 0, outer[0], outer[1])
            attend(1, [(mask_row, ((0, 0), (0, 2)))], r, False, 4, 1)

        for h in range(8):
            total = os_[r, h]
            att = (total[:HEAD] * (1.0 / total[HEAD : HEAD + 1])).astype(bf16)
            rows = pl.ds(h * HEAD, HEAD)
            full[r, c, rows] = jnp.where(mine_first, att[:, :TOK], att[:, TOK:])
            snd[r, rows] = jnp.where(mine_first, att[:, TOK:], att[:, :TOK])
        if COMM:
            att_to_peer(r, c).start()

    w_copies[3].wait()

    @pl.loop(0, 2)
    def _(t):
        r = 1 - t
        if COMM:
            att_to_peer(r, o).wait_recv()
        a = full[r].reshape(D, TOK)
        out_ref[r] = lax.dot_general(a, wo[...], TN, preferred_element_type=f32).astype(bf16)

    if COMM:
        for r in range(2):
            own_to_peer(r, c).wait_send()
            att_to_peer(r, c).wait_send()
        bias_to_peer(c).wait_send()

        @pl.when(has_next)
        def _():
            for r in range(2):
                for i in range(NC):
                    to_next(r, i).wait_send()

        for side in range(2):

            @pl.when(send_to[side])
            def _(side=side):
                for i in range(NC):
                    own_to_side(side, i).wait_send()

            @pl.when(gets_from[side])
            def _(side=side):
                for i in range(NC):
                    forward(0, 3 - 3 * side, i, c).wait_send()

        @pl.when(has_prev)
        def _():
            for side in range(2):
                for i in range(NC):
                    forward(1, 1 + side, i, c).wait_send()

                @pl.when(send_to[side])
                def _(side=side):
                    for i in range(NC):
                        prev_to_side(side, i).wait_send()

                @pl.when(gets_from[side])
                def _(side=side):
                    for i in range(NC):
                        forward(1, 3 - 3 * side, i, c).wait_send()


def on_device(frames_in, w_query, w_key, w_value, w_out, codes, counts):
    shape = frames_in.shape
    x = frames_in.reshape(2, TOK, D)
    bf16, f32 = jnp.bfloat16, jnp.float32
    dma = pltpu.SemaphoreType.DMA
    anywhere = pl.BlockSpec(memory_space=pl.ANY)
    scalars = pl.BlockSpec(memory_space=pltpu.SMEM)
    out = pl.pallas_call(
        kernel,
        out_shape=jax.ShapeDtypeStruct((2, TOK, D), bf16),
        in_specs=[anywhere] * 5 + [scalars] * 2,
        out_specs=pl.BlockSpec(memory_space=pltpu.VMEM),
        scratch_shapes=[
            pltpu.VMEM((2, 4, 2, TOK, D), bf16),
            pltpu.VMEM((D, HALF), bf16),
            pltpu.VMEM((D, HALF), bf16),
            pltpu.VMEM((D, HALF), bf16),
            pltpu.VMEM((D, D), bf16),
            pltpu.VMEM((HALF, D), bf16),
            pltpu.VMEM((2, 8, 2 * TOK, 128), bf16),
            pltpu.VMEM((2, 4, 4, 2 * TOK, 128), bf16),
            pltpu.VMEM((2, 4, 8, VROWS, 2 * TOK), bf16),
            pltpu.VMEM((2, 8, VROWS, 2 * TOK), f32),
            pltpu.VMEM((2, 8, 8, 2 * TOK), f32),
            pltpu.VMEM((2, 2, 3, 8, TOK), f32),
            pltpu.VMEM((2, HALF, TOK), bf16),
            pltpu.VMEM((2, 2, HALF, TOK), bf16),
            *([pltpu.VMEM((2 * TOK, 2 * TOK), f32)] * 8),
            dma((4,)),
            dma((2,)),
            dma((2,)),
            dma((2,)),
            dma((2 * NC,)),
            dma((2 * NC,)),
            dma((2 * NC,)),
            dma((2 * NC,)),
            dma((2 * NC,)),
            dma((2 * NC,)),
            dma((8 * NC,)),
            dma((8 * NC,)),
            dma((1,)),
            dma((1,)),
            dma((2,)),
            dma((2,)),
        ],
        compiler_params=pltpu.CompilerParams(
            vmem_limit_bytes=60 << 20,
            **(dict(collective_id=0, has_side_effects=True) if COMM else {}),
        ),
        cost_estimate=pl.CostEstimate(flops=12 * 10**9, bytes_accessed=8 << 20, transcendentals=6 << 20),
    )(x, w_query, w_key, w_value, w_out, codes, counts)
    return out.reshape(shape)


def solution(mesh):
    placed = (
        P("frame", "lat", "lon", None),
        P(),
        P(),
        P(),
        P(),
        P("frame", "lat", "lon", None),
        P("frame", "lat", "lon"),
    )
    return jax.shard_map(
        on_device,
        mesh=mesh,
        in_specs=placed,
        out_specs=P("frame", "lat", "lon", None),
        check_vma=False,
    )
```

```python
import functools

import jax
import jax.numpy as jnp
from jax import lax
from jax.experimental import pallas as pl
from jax.experimental.pallas import tpu as pltpu
from jax.sharding import PartitionSpec as P

HEADS = 16
HEAD = 64
TILE = 8
WIN = 9
D = 1024
HALF = D // 2
TOK = 128
NC = 4
CH = TOK // NC
VROWS = HEAD + 16
DEAD = -1e38
FLOOR = -1e30
MESH = pl.DeviceIdType.MESH
COMM = True
NT = (((1,), (1,)), ((), ()))
TN = (((0,), (0,)), ((), ()))


def kernel(
    x_ref, wq_ref, wk_ref, wv_ref, wo_ref, codes_hbm, counts_hbm, out_ref,
    codes_ref, counts_ref, xs, wq, wk, wv, wo, wvt, qz, ks, vt, os_, ms, bias, snd, full,
    s0, s1, s2, s3, s4, s5, s6, s7,
    w_sem, x_sem, c_sem,
    p_ss, p_rs, y_ss, y_rs, n0_ss, n0_rs, n1_ss, n1_rs, f_ss, f_rs, b_ss, b_rs, a_ss, a_rs,
):
    f32, bf16 = jnp.float32, jnp.bfloat16
    lat, c, frame = lax.axis_index("lat"), lax.axis_index("lon"), lax.axis_index("frame")
    nlat, nframe = lax.axis_size("lat"), lax.axis_size("frame")
    o = 1 - c
    ss = (s0, s1, s2, s3, s4, s5, s6, s7)
    has_n, has_s = lat > 0, lat < nlat - 1
    has_prev, has_next = frame > 0, frame < nframe - 1

    cols = pl.ds(pl.multiple_of(c * HALF, HALF), HALF)
    x_copies = [pltpu.make_async_copy(x_ref.at[r], xs.at[0, 1 + r, c], x_sem.at[r]) for r in range(2)]
    w_copies = [
        pltpu.make_async_copy(wv_ref.at[:, cols], wv, w_sem.at[0]),
        pltpu.make_async_copy(wk_ref.at[:, cols], wk, w_sem.at[1]),
        pltpu.make_async_copy(wq_ref.at[:, cols], wq, w_sem.at[2]),
        pltpu.make_async_copy(wo_ref, wo, w_sem.at[3]),
    ]
    c_copies = [
        pltpu.make_async_copy(codes_hbm, codes_ref, c_sem.at[0]),
        pltpu.make_async_copy(counts_hbm, counts_ref, c_sem.at[1]),
    ]

    def remote(src, dst, ss, rs, dev):
        return pltpu.make_async_remote_copy(
            src_ref=src, dst_ref=dst, send_sem=ss, recv_sem=rs, device_id=dev, device_id_type=MESH
        )

    def part(i):
        return pl.ds(pl.multiple_of(i * CH, CH), CH)

    def own_to_peer(r, lon):
        return remote(x_ref.at[r], xs.at[0, 1 + r, lon], p_ss.at[r], p_rs.at[r], {"lon": o})

    def to_next(r, i):
        k = r * NC + i
        return remote(x_ref.at[r, part(i)], xs.at[1, 1 + r, c, part(i)], y_ss.at[k], y_rs.at[k], {"frame": frame + 1})

    def side_dev(side):
        return {"lat": lat - 1 + 2 * side}

    def own_to_side(side, i):
        k = side * NC + i
        return remote(
            x_ref.at[side, part(i)], xs.at[0, 3 - 3 * side, c, part(i)], n0_ss.at[k], n0_rs.at[k], side_dev(side)
        )

    def prev_to_side(side, i):
        k = side * NC + i
        return remote(
            xs.at[1, 1 + side, c, part(i)], xs.at[1, 3 - 3 * side, c, part(i)], n1_ss.at[k], n1_rs.at[k], side_dev(side)
        )

    def forward(fr, row, i, lon):
        k = (fr * 4 + row) * NC + i
        block = xs.at[fr, row, lon, part(i)]
        return remote(block, block, f_ss.at[k], f_rs.at[k], {"lon": o})

    def bias_to_peer(lon):
        return remote(bias.at[lon], bias.at[lon], b_ss.at[0], b_rs.at[0], {"lon": o})

    def att_to_peer(r, lon):
        return remote(snd.at[r], full.at[r, lon], a_ss.at[r], a_rs.at[r], {"lon": o})

    send_to = (has_n, has_s)
    gets_from = (has_s, has_n)

    if COMM:
        barrier = pltpu.get_barrier_semaphore()

        def greet(dev):
            pl.semaphore_signal(barrier, inc=1, device_id=dev, device_id_type=MESH)

        greet({"lon": o})
        pl.when(has_n)(lambda: greet({"lat": lat - 1}))
        pl.when(has_s)(lambda: greet({"lat": lat + 1}))
        pl.when(has_prev)(lambda: greet({"frame": frame - 1}))
        pl.when(has_next)(lambda: greet({"frame": frame + 1}))

    for copy in x_copies + c_copies + w_copies:
        copy.start()

    if COMM:
        greeted = (
            1
            + has_n.astype(jnp.int32)
            + has_s.astype(jnp.int32)
            + has_prev.astype(jnp.int32)
            + has_next.astype(jnp.int32)
        )
        pl.semaphore_wait(barrier, greeted)
        for r in range(2):
            own_to_peer(r, c).start()

        @pl.when(has_next)
        def _():
            for i in range(NC):
                to_next(0, i).start()

        for side in range(2):

            @pl.when(send_to[side])
            def _(side=side):
                for i in range(NC):
                    own_to_side(side, i).start()

        @pl.when(has_next)
        def _():
            for i in range(NC):
                to_next(1, i).start()


    ri = lax.broadcasted_iota(jnp.int32, (8, TOK), 0)
    li = lax.broadcasted_iota(jnp.int32, (8, TOK), 1)
    second = (li // TILE) % 2 == 1
    gcol = 2 * c + (li // TILE) % 2
    wcol = (ri - gcol + 5) % 4
    for copy in c_copies:
        copy.wait()
    outer = [jnp.where(has_n, 0, 3), jnp.where(has_s, 3, 0)]
    for r in range(2):
        first = jnp.minimum(jnp.maximum(2 * lat + r - 1, 0), 2 * nlat - 3) - 2 * lat + 1
        cnt = jnp.where(second, counts_ref[0, r, 1], counts_ref[0, r, 0])
        for slot in range(3):
            ext = outer[r] if slot == 0 else slot
            want = jnp.where(jnp.logical_and(wcol < 3, ri < 4), 3 * (ext - first) + wcol, -1)
            live = jnp.zeros((8, TOK), f32)
            for j in range(WIN):
                code = jnp.where(second, codes_ref[0, r, 1, j], codes_ref[0, r, 0, j])
                hit = jnp.logical_and(code == want, j < cnt)
                live = jnp.where(hit, 1.0, live)
            bias[c, r, slot] = jnp.where(live > 0.5, 0.0, DEAD)
    if COMM:
        bias_to_peer(c).start()
    vt[:, :, :, :, HEAD:, :] = jnp.ones((2, 4, 2, 8, VROWS - HEAD, TOK), bf16)
    w_copies[0].wait()
    wvt[...] = wv[...].T

    def quarter(i):
        return [i * (NC // 4) + k for k in range(NC // 4)]

    def pump_own_sides(q):
        if not COMM:
            return
        for side in range(2):

            @pl.when(gets_from[side])
            def _(side=side):
                for i in quarter(q):
                    own_to_side(side, i).wait_recv()
                    forward(0, 3 - 3 * side, i, c).start()

    def pump_prev(r, q):
        if not COMM:
            return

        @pl.when(has_prev)
        def _():
            for i in quarter(q):
                to_next(r, i).wait_recv()

                @pl.when(send_to[r])
                def _():
                    prev_to_side(r, i).start()

                forward(1, 1 + r, i, c).start()

    def pump_prev_side(side, q):
        if COMM:
            for i in quarter(q):
                prev_to_side(side, i).wait_recv()
                forward(1, 3 - 3 * side, i, c).start()

    def await_forward(fr, row):
        if COMM:
            for i in range(NC):
                forward(fr, row, i, o).wait_recv()

    def project(fr, pieces):
        x = jnp.concatenate([xs[fr, row, lon] for row, lon in pieces], axis=0)
        key = jnp.dot(x, wk[...], preferred_element_type=f32).astype(bf16)
        value = lax.dot_general(wvt[...], x, NT, preferred_element_type=f32).astype(bf16)
        for u, (row, lon) in enumerate(pieces):
            for pair in range(4):
                ks[fr, row, lon, pair] = key[u * TOK : (u + 1) * TOK, pair * 128 : (pair + 1) * 128]
            vt[fr, row, lon, :, :HEAD, :] = value[:, u * TOK : (u + 1) * TOK].reshape(8, HEAD, TOK)
        return x

    def attend(blocks, r, first, group, ahead):
        n = len(blocks)
        masks = []
        for _, _, slot in blocks:
            rows = jnp.concatenate([bias[0, r, slot], bias[1, r, slot]], axis=1)
            masks.append([rows[2 * u : 2 * u + 2].reshape(2, 1, 2 * TOK) for u in range(2)])

        def scores(h):
            best = None
            for k, (fr, row, _) in enumerate(blocks):
                key = jnp.concatenate([ks[fr, row, 0, h // 2], ks[fr, row, 1, h // 2]], axis=0)
                s = lax.dot_general(key, qz[r, h], NT, preferred_element_type=f32)
                ss[(h * n + k) % 8][...] = s
                s = s.reshape(2, TILE, 2, TILE, 2 * TOK)
                for u in range(2):
                    top = jnp.max(jnp.max(s[u], axis=0) + masks[k][u], axis=0)
                    best = top if best is None else jnp.maximum(best, top)
            m = jnp.maximum(jnp.max(best, axis=0, keepdims=True), FLOOR)
            if first:
                return m, None
            m_old = ms[r, h, :1]
            return jnp.maximum(m, m_old), m_old

        def values(h, m, m_old):
            total = None
            for k, (fr, row, _) in enumerate(blocks):
                s = ss[(h * n + k) % 8][...].reshape(2, TILE, 2, TILE, 2 * TOK)
                p = [jnp.exp(s[u] + (masks[k][u] - m)[None]).reshape(TOK, 2 * TOK).astype(bf16) for u in range(2)]
                value = jnp.concatenate([vt[fr, row, 0, h], vt[fr, row, 1, h]], axis=1)
                t = jnp.dot(value, jnp.concatenate(p, axis=0), preferred_element_type=f32)
                total = t if total is None else total + t
            if not first:
                total = total + os_[r, h] * jnp.exp(m_old - m)
            os_[r, h] = total
            ms[r, h] = jnp.broadcast_to(m, (8, 2 * TOK))

        steps = 8 // group
        state = {}
        for g in range(steps + ahead):
            if g < steps:
                for h in range(g * group, (g + 1) * group):
                    state[h] = scores(h)
            if g >= ahead:
                for h in range((g - ahead) * group, (g - ahead + 1) * group):
                    values(h, *state.pop(h))

    low = lax.broadcasted_iota(jnp.int32, (TOK, 128), 1) < HEAD
    for copy in x_copies:
        copy.wait()
    w_copies[1].wait()
    w_copies[2].wait()

    @pl.loop(0, 2)
    def _(t):
        lon = jnp.where(t == 0, c, o)

        @pl.when(t == 1)
        def _():
            if COMM:
                for r in range(2):
                    own_to_peer(r, o).wait_recv()
                bias_to_peer(o).wait_recv()

        x = project(0, [(1, lon), (2, lon)])
        query = jnp.dot(x, wq[...], preferred_element_type=f32).astype(bf16).astype(f32) * 0.125
        place = pl.ds(pl.multiple_of(lon * TOK, TOK), TOK)
        for r in range(2):
            for pair in range(4):
                q = query[r * TOK : (r + 1) * TOK, pair * 128 : (pair + 1) * 128]
                qz[r, 2 * pair, place] = jnp.where(low, q, 0.0).astype(bf16)
                qz[r, 2 * pair + 1, place] = jnp.where(low, 0.0, q).astype(bf16)

    @pl.loop(0, 2)
    def _(r):
        pump_prev(0, r)
        pump_own_sides(r)
        attend([(0, 1, 1), (0, 2, 2)], r, True, 2, 1)

    pump_prev(0, 2)
    pump_own_sides(2)
    pump_prev(0, 3)
    pump_own_sides(3)

    project(0, [(0, c), (3, c)])
    pump_prev(1, 0)

    @pl.when(has_prev)
    def _():
        await_forward(1, 1)
        project(1, [(1, 0), (1, 1)])

    pump_prev(1, 1)
    for side in range(2):
        pl.when(gets_from[side])(functools.partial(await_forward, 0, 3 - 3 * side))
    project(0, [(0, o), (3, o)])

    def outer_of(r):
        return jnp.where(r == 0, outer[0], outer[1])

    @pl.loop(0, 2)
    def _(r):
        pump_prev(1, 2 + r)

        @pl.when(has_prev)
        def _():
            attend([(0, outer_of(r), 0), (1, 1, 1)], r, False, 2, 1)

        @pl.when(jnp.logical_not(has_prev))
        def _():
            attend([(0, outer_of(r), 0)], r, False, 4, 1)

    both_sides = jnp.logical_and(has_n, has_s)

    @pl.when(has_prev)
    def _():
        @pl.when(has_s)
        def _():
            for i in range(4):
                pump_prev_side(0, i)

        await_forward(1, 2)
        project(1, [(2, 0), (2, 1)])

        @pl.when(has_n)
        def _():
            for i in range(3):
                pump_prev_side(1, i)

        attend([(1, 2, 2)], 0, False, 4, 1)
        pl.when(jnp.logical_not(has_s))(lambda: pump_prev_side(1, 3))
        row = jnp.where(has_s, 3, 0)
        await_forward(1, row)
        project(1, [(row, 0), (row, 1)])
        attend([(1, 2, 2), (1, outer[1], 0)], 1, False, 2, 1)

    mine_first = c == 0

    def finish(r):
        for h in range(8):
            total = os_[r, h]
            att = (total[:HEAD] * (1.0 / total[HEAD : HEAD + 1])).astype(bf16)
            rows = pl.ds(h * HEAD, HEAD)
            full[r, c, rows] = jnp.where(mine_first, att[:, :TOK], att[:, TOK:])
            snd[r, rows] = jnp.where(mine_first, att[:, TOK:], att[:, :TOK])
        if COMM:
            att_to_peer(r, c).start()

    def put_out(r):
        if COMM:
            att_to_peer(r, o).wait_recv()
        a = full[r].reshape(D, TOK)
        out_ref[r] = lax.dot_general(a, wo[...], TN, preferred_element_type=f32).astype(bf16)

    finish(1)

    @pl.when(has_prev)
    def _():
        @pl.when(both_sides)
        def _():
            pump_prev_side(1, 3)
            await_forward(1, 0)
            project(1, [(0, 0), (0, 1)])

        attend([(1, outer[0], 0)], 0, False, 4, 1)

    finish(0)
    w_copies[3].wait()

    @pl.loop(0, 2)
    def _(t):
        put_out(1 - t)

    if COMM:
        for r in range(2):
            own_to_peer(r, c).wait_send()
            att_to_peer(r, c).wait_send()
        bias_to_peer(c).wait_send()

        @pl.when(has_next)
        def _():
            for r in range(2):
                for i in range(NC):
                    to_next(r, i).wait_send()

        for side in range(2):

            @pl.when(send_to[side])
            def _(side=side):
                for i in range(NC):
                    own_to_side(side, i).wait_send()

            @pl.when(gets_from[side])
            def _(side=side):
                for i in range(NC):
                    forward(0, 3 - 3 * side, i, c).wait_send()

        @pl.when(has_prev)
        def _():
            for side in range(2):
                for i in range(NC):
                    forward(1, 1 + side, i, c).wait_send()

                @pl.when(send_to[side])
                def _(side=side):
                    for i in range(NC):
                        prev_to_side(side, i).wait_send()

                @pl.when(gets_from[side])
                def _(side=side):
                    for i in range(NC):
                        forward(1, 3 - 3 * side, i, c).wait_send()


def on_device(frames_in, w_query, w_key, w_value, w_out, codes, counts):
    shape = frames_in.shape
    x = frames_in.reshape(2, TOK, D)
    bf16, f32 = jnp.bfloat16, jnp.float32
    dma = pltpu.SemaphoreType.DMA
    out = pl.pallas_call(
        kernel,
        out_shape=jax.ShapeDtypeStruct((2, TOK, D), bf16),
        in_specs=[pl.BlockSpec(memory_space=pltpu.HBM)] * 7,
        out_specs=pl.BlockSpec(memory_space=pltpu.VMEM),
        scratch_shapes=[
            pltpu.SMEM((1, 2, 2, WIN), jnp.int32),
            pltpu.SMEM((1, 2, 2), jnp.int32),
            pltpu.VMEM((2, 4, 2, TOK, D), bf16),
            pltpu.VMEM((D, HALF), bf16),
            pltpu.VMEM((D, HALF), bf16),
            pltpu.VMEM((D, HALF), bf16),
            pltpu.VMEM((D, D), bf16),
            pltpu.VMEM((HALF, D), bf16),
            pltpu.VMEM((2, 8, 2 * TOK, 128), bf16),
            pltpu.VMEM((2, 4, 2, 4, TOK, 128), bf16),
            pltpu.VMEM((2, 4, 2, 8, VROWS, TOK), bf16),
            pltpu.VMEM((2, 8, VROWS, 2 * TOK), f32),
            pltpu.VMEM((2, 8, 8, 2 * TOK), f32),
            pltpu.VMEM((2, 2, 3, 8, TOK), f32),
            pltpu.VMEM((2, HALF, TOK), bf16),
            pltpu.VMEM((2, 2, HALF, TOK), bf16),
            *([pltpu.VMEM((2 * TOK, 2 * TOK), f32)] * 8),
            dma((4,)),
            dma((2,)),
            dma((2,)),
            dma((2,)),
            dma((2,)),
            dma((2 * NC,)),
            dma((2 * NC,)),
            dma((2 * NC,)),
            dma((2 * NC,)),
            dma((2 * NC,)),
            dma((2 * NC,)),
            dma((8 * NC,)),
            dma((8 * NC,)),
            dma((1,)),
            dma((1,)),
            dma((2,)),
            dma((2,)),
        ],
        compiler_params=pltpu.CompilerParams(
            vmem_limit_bytes=44 << 20,
            **(dict(collective_id=0, has_side_effects=True) if COMM else {}),
        ),
        cost_estimate=pl.CostEstimate(flops=12 * 10**9, bytes_accessed=8 << 20, transcendentals=6 << 20),
    )(*[pltpu.with_memory_space_constraint(v, pltpu.HBM) for v in (x, w_query, w_key, w_value, w_out, codes, counts)])
    return out.reshape(shape)


def solution(mesh):
    placed = (
        P("frame", "lat", "lon", None),
        P(),
        P(),
        P(),
        P(),
        P("frame", "lat", "lon", None),
        P("frame", "lat", "lon"),
    )
    return jax.shard_map(
        on_device,
        mesh=mesh,
        in_specs=placed,
        out_specs=P("frame", "lat", "lon", None),
        check_vma=False,
    )
```

```python
import functools

import jax
import jax.numpy as jnp
from jax import lax
from jax.experimental import pallas as pl
from jax.experimental.pallas import tpu as pltpu
from jax.sharding import PartitionSpec as P

HEADS = 16
HEAD = 64
TILE = 8
WIN = 9
D = 1024
HALF = D // 2
TOK = 128
NC = 4
BIG, SMALL = 32, 32
VROWS = HEAD + 16
DEAD = -1e38
FLOOR = -1e30
MESH = pl.DeviceIdType.MESH
COMM = True
NT = (((1,), (1,)), ((), ()))
TN = (((0,), (0,)), ((), ()))


def kernel(
    x_ref, wq_ref, wk_ref, wv_ref, wo_ref, codes_hbm, counts_hbm, out_ref,
    codes_ref, counts_ref, xs, wq, wk, wv, wo, wvt, qz, ks, vt, os_, ms, bias, snd, full,
    s0, s1, s2, s3, s4, s5, s6, s7,
    w_sem, x_sem, c_sem,
    p_ss, p_rs, y_ss, y_rs, n0_ss, n0_rs, n1_ss, n1_rs, f_ss, f_rs, b_ss, b_rs, a_ss, a_rs,
):
    f32, bf16 = jnp.float32, jnp.bfloat16
    lat, c, frame = lax.axis_index("lat"), lax.axis_index("lon"), lax.axis_index("frame")
    nlat, nframe = lax.axis_size("lat"), lax.axis_size("frame")
    o = 1 - c
    ss = (s0, s1, s2, s3, s4, s5, s6, s7)
    has_n, has_s = lat > 0, lat < nlat - 1
    has_prev, has_next = frame > 0, frame < nframe - 1

    cols = pl.ds(pl.multiple_of(c * HALF, HALF), HALF)
    x_copies = [pltpu.make_async_copy(x_ref.at[r], xs.at[0, 1 + r, c], x_sem.at[r]) for r in range(2)]
    w_copies = [
        pltpu.make_async_copy(wv_ref.at[:, cols], wv, w_sem.at[0]),
        pltpu.make_async_copy(wk_ref.at[:, cols], wk, w_sem.at[1]),
        pltpu.make_async_copy(wq_ref.at[:, cols], wq, w_sem.at[2]),
        pltpu.make_async_copy(wo_ref, wo, w_sem.at[3]),
    ]
    c_copies = [
        pltpu.make_async_copy(codes_hbm, codes_ref, c_sem.at[0]),
        pltpu.make_async_copy(counts_hbm, counts_ref, c_sem.at[1]),
    ]

    def remote(src, dst, ss, rs, dev):
        return pltpu.make_async_remote_copy(
            src_ref=src, dst_ref=dst, send_sem=ss, recv_sem=rs, device_id=dev, device_id_type=MESH
        )

    def part(i, size):
        start = BIG * i if size == BIG else 2 * BIG + SMALL * (i - 2)
        return pl.ds(pl.multiple_of(start, 16), size)

    def pieces():
        return [(i, BIG if i < 2 else SMALL) for i in range(NC)]

    def own_to_peer(r, lon):
        return remote(x_ref.at[r], xs.at[0, 1 + r, lon], p_ss.at[r], p_rs.at[r], {"lon": o})

    def to_next(r, i, size):
        k = r * NC + i
        return remote(x_ref.at[r, part(i, size)], xs.at[1, 1 + r, c, part(i, size)], y_ss.at[k], y_rs.at[k], {"frame": frame + 1})

    def side_dev(side):
        return {"lat": lat - 1 + 2 * side}

    def own_to_side(side, i, size):
        k = side * NC + i
        return remote(
            x_ref.at[side, part(i, size)], xs.at[0, 3 - 3 * side, c, part(i, size)], n0_ss.at[k], n0_rs.at[k], side_dev(side)
        )

    def prev_to_side(side, i, size):
        k = side * NC + i
        return remote(
            xs.at[1, 1 + side, c, part(i, size)], xs.at[1, 3 - 3 * side, c, part(i, size)], n1_ss.at[k], n1_rs.at[k], side_dev(side)
        )

    def forward(fr, row, i, size, lon):
        k = (fr * 4 + row) * NC + i
        block = xs.at[fr, row, lon, part(i, size)]
        return remote(block, block, f_ss.at[k], f_rs.at[k], {"lon": o})

    def bias_to_peer(lon):
        return remote(bias.at[lon], bias.at[lon], b_ss.at[0], b_rs.at[0], {"lon": o})

    def att_to_peer(r, lon):
        return remote(snd.at[r], full.at[r, lon], a_ss.at[r], a_rs.at[r], {"lon": o})

    send_to = (has_n, has_s)
    gets_from = (has_s, has_n)
    ra = jnp.where(lat % 4 == 3, 1, 0)
    rb = 1 - ra

    if COMM:
        barrier = pltpu.get_barrier_semaphore()

        def greet(dev):
            pl.semaphore_signal(barrier, inc=1, device_id=dev, device_id_type=MESH)

        greet({"lon": o})
        pl.when(has_n)(lambda: greet({"lat": lat - 1}))
        pl.when(has_s)(lambda: greet({"lat": lat + 1}))
        pl.when(has_prev)(lambda: greet({"frame": frame - 1}))
        pl.when(has_next)(lambda: greet({"frame": frame + 1}))

    for copy in x_copies + c_copies + w_copies:
        copy.start()

    if COMM:
        greeted = (
            1
            + has_n.astype(jnp.int32)
            + has_s.astype(jnp.int32)
            + has_prev.astype(jnp.int32)
            + has_next.astype(jnp.int32)
        )
        pl.semaphore_wait(barrier, greeted)
        for r in range(2):
            own_to_peer(r, c).start()

        @pl.when(has_next)
        def _():
            for i, size in pieces():
                to_next(ra, i, size).start()

        for side in range(2):

            @pl.when(send_to[side])
            def _(side=side):
                for i, size in pieces():
                    own_to_side(side, i, size).start()

        @pl.when(has_next)
        def _():
            for i, size in pieces():
                to_next(rb, i, size).start()

    ri = lax.broadcasted_iota(jnp.int32, (8, TOK), 0)
    li = lax.broadcasted_iota(jnp.int32, (8, TOK), 1)
    second = (li // TILE) % 2 == 1
    gcol = 2 * c + (li // TILE) % 2
    wcol = (ri - gcol + 5) % 4
    for copy in c_copies:
        copy.wait()
    outer = [jnp.where(has_n, 0, 3), jnp.where(has_s, 3, 0)]
    for r in range(2):
        first = jnp.minimum(jnp.maximum(2 * lat + r - 1, 0), 2 * nlat - 3) - 2 * lat + 1
        cnt = jnp.where(second, counts_ref[0, r, 1], counts_ref[0, r, 0])
        for slot in range(3):
            ext = outer[r] if slot == 0 else slot
            want = jnp.where(jnp.logical_and(wcol < 3, ri < 4), 3 * (ext - first) + wcol, -1)
            live = jnp.zeros((8, TOK), f32)
            for j in range(WIN):
                code = jnp.where(second, codes_ref[0, r, 1, j], codes_ref[0, r, 0, j])
                hit = jnp.logical_and(code == want, j < cnt)
                live = jnp.where(hit, 1.0, live)
            bias[c, r, slot] = jnp.where(live > 0.5, 0.0, DEAD)
    if COMM:
        bias_to_peer(c).start()
    vt[:, :, :, :, HEAD:, :] = jnp.ones((2, 4, 2, 8, VROWS - HEAD, TOK), bf16)
    w_copies[0].wait()
    wvt[...] = wv[...].T

    def pump_own_sides(i, size):
        if not COMM:
            return
        for side in range(2):

            @pl.when(gets_from[side])
            def _(side=side):
                own_to_side(side, i, size).wait_recv()
                forward(0, 3 - 3 * side, i, size, c).start()

    def pump_prev(r, i, size):
        if not COMM:
            return

        @pl.when(has_prev)
        def _():
            to_next(r, i, size).wait_recv()

            @pl.when(jnp.where(r == 0, has_n, has_s))
            def _():
                prev_to_side(r, i, size).start()

            forward(1, 1 + r, i, size, c).start()

    def pump_prev_side(side, i, size):
        if not COMM:
            return

        @pl.when(gets_from[side])
        def _():
            prev_to_side(side, i, size).wait_recv()
            forward(1, 3 - 3 * side, i, size, c).start()

    def await_forward(fr, row):
        if COMM:
            for i, size in pieces():
                forward(fr, row, i, size, o).wait_recv()

    def project(fr, pieces):
        x = jnp.concatenate([xs[fr, row, lon] for row, lon in pieces], axis=0)
        key = jnp.dot(x, wk[...], preferred_element_type=f32).astype(bf16)
        value = lax.dot_general(wvt[...], x, NT, preferred_element_type=f32).astype(bf16)
        for u, (row, lon) in enumerate(pieces):
            for pair in range(4):
                ks[fr, row, lon, pair] = key[u * TOK : (u + 1) * TOK, pair * 128 : (pair + 1) * 128]
            vt[fr, row, lon, :, :HEAD, :] = value[:, u * TOK : (u + 1) * TOK].reshape(8, HEAD, TOK)
        return x

    def attend(blocks, r, first, group, ahead):
        n = len(blocks)
        masks = []
        for _, _, slot in blocks:
            rows = jnp.concatenate([bias[0, r, slot], bias[1, r, slot]], axis=1)
            masks.append([rows[2 * u : 2 * u + 2].reshape(2, 1, 2 * TOK) for u in range(2)])

        def scores(h):
            best = None
            for k, (fr, row, _) in enumerate(blocks):
                key = jnp.concatenate([ks[fr, row, 0, h // 2], ks[fr, row, 1, h // 2]], axis=0)
                s = lax.dot_general(key, qz[r, h], NT, preferred_element_type=f32)
                ss[(h * n + k) % 8][...] = s
                s = s.reshape(2, TILE, 2, TILE, 2 * TOK)
                for u in range(2):
                    top = jnp.max(jnp.max(s[u], axis=0) + masks[k][u], axis=0)
                    best = top if best is None else jnp.maximum(best, top)
            m = jnp.maximum(jnp.max(best, axis=0, keepdims=True), FLOOR)
            if first:
                return m, None
            m_old = ms[r, h, :1]
            return jnp.maximum(m, m_old), m_old

        def values(h, m, m_old):
            total = None
            for k, (fr, row, _) in enumerate(blocks):
                s = ss[(h * n + k) % 8][...].reshape(2, TILE, 2, TILE, 2 * TOK)
                p = [jnp.exp(s[u] + (masks[k][u] - m)[None]).reshape(TOK, 2 * TOK).astype(bf16) for u in range(2)]
                value = jnp.concatenate([vt[fr, row, 0, h], vt[fr, row, 1, h]], axis=1)
                t = jnp.dot(value, jnp.concatenate(p, axis=0), preferred_element_type=f32)
                total = t if total is None else total + t
            if not first:
                total = total + os_[r, h] * jnp.exp(m_old - m)
            os_[r, h] = total
            ms[r, h] = jnp.broadcast_to(m, (8, 2 * TOK))

        steps = 8 // group
        state = {}
        for g in range(steps + ahead):
            if g < steps:
                for h in range(g * group, (g + 1) * group):
                    state[h] = scores(h)
            if g >= ahead:
                for h in range((g - ahead) * group, (g - ahead + 1) * group):
                    values(h, *state.pop(h))

    low = lax.broadcasted_iota(jnp.int32, (TOK, 128), 1) < HEAD
    for copy in x_copies:
        copy.wait()
    w_copies[1].wait()
    w_copies[2].wait()

    @pl.loop(0, 2)
    def _(t):
        lon = jnp.where(t == 0, c, o)

        @pl.when(t == 1)
        def _():
            if COMM:
                for r in range(2):
                    own_to_peer(r, o).wait_recv()
                bias_to_peer(o).wait_recv()

        x = project(0, [(1, lon), (2, lon)])
        query = jnp.dot(x, wq[...], preferred_element_type=f32).astype(bf16).astype(f32) * 0.125
        place = pl.ds(pl.multiple_of(lon * TOK, TOK), TOK)
        for r in range(2):
            for pair in range(4):
                q = query[r * TOK : (r + 1) * TOK, pair * 128 : (pair + 1) * 128]
                qz[r, 2 * pair, place] = jnp.where(low, q, 0.0).astype(bf16)
                qz[r, 2 * pair + 1, place] = jnp.where(low, 0.0, q).astype(bf16)

    @pl.loop(0, 2)
    def _(r):
        pump_prev(ra, r, BIG)
        pump_own_sides(r, BIG)
        attend([(0, 1, 1), (0, 2, 2)], r, True, 2, 1)

    for i in range(2, 4):
        pump_prev(ra, i, SMALL)
        pump_own_sides(i, SMALL)

    project(0, [(0, c), (3, c)])
    pump_prev(rb, 0, BIG)

    @pl.when(has_prev)
    def _():
        await_forward(1, 1 + ra)
        project(1, [(1 + ra, 0), (1 + ra, 1)])
        pump_prev(rb, 1, BIG)

    for side in range(2):
        pl.when(gets_from[side])(functools.partial(await_forward, 0, 3 - 3 * side))
    project(0, [(0, o), (3, o)])

    def outer_of(r):
        return jnp.where(r == 0, outer[0], outer[1])

    @pl.loop(0, 2)
    def _(r):
        pump_prev(rb, 2 + r, SMALL)

        @pl.when(has_prev)
        def _():
            attend([(0, outer_of(r), 0), (1, 1 + ra, 1 + ra)], r, False, 2, 1)

        @pl.when(jnp.logical_not(has_prev))
        def _():
            attend([(0, outer_of(r), 0)], r, False, 4, 1)

    both_sides = jnp.logical_and(has_n, has_s)

    @pl.when(has_prev)
    def _():
        await_forward(1, 1 + rb)
        project(1, [(1 + rb, 0), (1 + rb, 1)])
        for side in range(2):
            for i in range(2):
                pump_prev_side(side, i, BIG)
        @pl.loop(0, 2)
        def _(r):
            attend([(1, 1 + rb, 1 + rb)], r, False, 4, 1)

        for i in range(2, 4):
            for side in range(2):
                pump_prev_side(side, i, SMALL)

        project(1, [(0, c), (3, c)])
        for side in range(2):
            pl.when(gets_from[side])(functools.partial(await_forward, 1, 3 - 3 * side))
        project(1, [(0, o), (3, o)])
        attend([(1, outer[1], 0)], 1, False, 4, 1)

    mine_first = c == 0

    def finish(r):
        for h in range(8):
            total = os_[r, h]
            att = (total[:HEAD] * (1.0 / total[HEAD : HEAD + 1])).astype(bf16)
            rows = pl.ds(h * HEAD, HEAD)
            full[r, c, rows] = jnp.where(mine_first, att[:, :TOK], att[:, TOK:])
            snd[r, rows] = jnp.where(mine_first, att[:, TOK:], att[:, :TOK])
        if COMM:
            att_to_peer(r, c).start()

    def put_out(r):
        if COMM:
            att_to_peer(r, o).wait_recv()
        a = full[r].reshape(D, TOK)
        out_ref[r] = lax.dot_general(a, wo[...], TN, preferred_element_type=f32).astype(bf16)

    finish(1)

    @pl.when(has_prev)
    def _():
        attend([(1, outer[0], 0)], 0, False, 4, 1)

    finish(0)
    w_copies[3].wait()

    @pl.loop(0, 2)
    def _(t):
        put_out(1 - t)

    if COMM:
        for r in range(2):
            own_to_peer(r, c).wait_send()
            att_to_peer(r, c).wait_send()
        bias_to_peer(c).wait_send()

        @pl.when(has_next)
        def _():
            for r in range(2):
                for i, size in pieces():
                    to_next(r, i, size).wait_send()

        for side in range(2):

            @pl.when(send_to[side])
            def _(side=side):
                for i, size in pieces():
                    own_to_side(side, i, size).wait_send()

            @pl.when(gets_from[side])
            def _(side=side):
                for i, size in pieces():
                    forward(0, 3 - 3 * side, i, size, c).wait_send()

        @pl.when(has_prev)
        def _():
            for side in range(2):
                for i, size in pieces():
                    forward(1, 1 + side, i, size, c).wait_send()

                @pl.when(send_to[side])
                def _(side=side):
                    for i, size in pieces():
                        prev_to_side(side, i, size).wait_send()

                @pl.when(gets_from[side])
                def _(side=side):
                    for i, size in pieces():
                        forward(1, 3 - 3 * side, i, size, c).wait_send()


def on_device(frames_in, w_query, w_key, w_value, w_out, codes, counts):
    shape = frames_in.shape
    x = frames_in.reshape(2, TOK, D)
    bf16, f32 = jnp.bfloat16, jnp.float32
    dma = pltpu.SemaphoreType.DMA
    out = pl.pallas_call(
        kernel,
        out_shape=jax.ShapeDtypeStruct((2, TOK, D), bf16),
        in_specs=[pl.BlockSpec(memory_space=pltpu.HBM)] * 7,
        out_specs=pl.BlockSpec(memory_space=pltpu.VMEM),
        scratch_shapes=[
            pltpu.SMEM((1, 2, 2, WIN), jnp.int32),
            pltpu.SMEM((1, 2, 2), jnp.int32),
            pltpu.VMEM((2, 4, 2, TOK, D), bf16),
            pltpu.VMEM((D, HALF), bf16),
            pltpu.VMEM((D, HALF), bf16),
            pltpu.VMEM((D, HALF), bf16),
            pltpu.VMEM((D, D), bf16),
            pltpu.VMEM((HALF, D), bf16),
            pltpu.VMEM((2, 8, 2 * TOK, 128), bf16),
            pltpu.VMEM((2, 4, 2, 4, TOK, 128), bf16),
            pltpu.VMEM((2, 4, 2, 8, VROWS, TOK), bf16),
            pltpu.VMEM((2, 8, VROWS, 2 * TOK), f32),
            pltpu.VMEM((2, 8, 8, 2 * TOK), f32),
            pltpu.VMEM((2, 2, 3, 8, TOK), f32),
            pltpu.VMEM((2, HALF, TOK), bf16),
            pltpu.VMEM((2, 2, HALF, TOK), bf16),
            *([pltpu.VMEM((2 * TOK, 2 * TOK), f32)] * 8),
            dma((4,)),
            dma((2,)),
            dma((2,)),
            dma((2,)),
            dma((2,)),
            dma((2 * NC,)),
            dma((2 * NC,)),
            dma((2 * NC,)),
            dma((2 * NC,)),
            dma((2 * NC,)),
            dma((2 * NC,)),
            dma((8 * NC,)),
            dma((8 * NC,)),
            dma((1,)),
            dma((1,)),
            dma((2,)),
            dma((2,)),
        ],
        compiler_params=pltpu.CompilerParams(
            vmem_limit_bytes=44 << 20,
            **(dict(collective_id=0, has_side_effects=True) if COMM else {}),
        ),
        cost_estimate=pl.CostEstimate(flops=12 * 10**9, bytes_accessed=8 << 20, transcendentals=6 << 20),
    )(*[pltpu.with_memory_space_constraint(v, pltpu.HBM) for v in (x, w_query, w_key, w_value, w_out, codes, counts)])
    return out.reshape(shape)


def solution(mesh):
    placed = (
        P("frame", "lat", "lon", None),
        P(),
        P(),
        P(),
        P(),
        P("frame", "lat", "lon", None),
        P("frame", "lat", "lon"),
    )
    return jax.shard_map(
        on_device,
        mesh=mesh,
        in_specs=placed,
        out_specs=P("frame", "lat", "lon", None),
        check_vma=False,
    )
```

```python
import functools

import jax
import jax.numpy as jnp
from jax import lax
from jax.experimental import pallas as pl
from jax.experimental.pallas import tpu as pltpu
from jax.sharding import PartitionSpec as P

HEADS = 16
HEAD = 64
TILE = 8
WIN = 9
D = 1024
HALF = D // 2
TOK = 128
NC = 4
BIG, SMALL = 32, 32
VROWS = HEAD + 16
DEAD = -1e38
FLOOR = -1e30
MESH = pl.DeviceIdType.MESH
COMM = True
NT = (((1,), (1,)), ((), ()))
TN = (((0,), (0,)), ((), ()))


def kernel(
    x_ref, wq_ref, wk_ref, wv_ref, wo_ref, codes_hbm, counts_hbm, out_ref,
    codes_ref, counts_ref, xs, wq, wk, wv, wo, wvt, qz, ks, vt, os_, ms, bias, snd, full, part_out,
    s0, s1, s2, s3, s4, s5, s6, s7,
    w_sem, x_sem, c_sem,
    p_ss, p_rs, y_ss, y_rs, n0_ss, n0_rs, n1_ss, n1_rs, f_ss, f_rs, b_ss, b_rs, a_ss, a_rs,
):
    f32, bf16 = jnp.float32, jnp.bfloat16
    lat, c, frame = lax.axis_index("lat"), lax.axis_index("lon"), lax.axis_index("frame")
    nlat, nframe = lax.axis_size("lat"), lax.axis_size("frame")
    o = 1 - c
    ss = (s0, s1, s2, s3, s4, s5, s6, s7)
    has_n, has_s = lat > 0, lat < nlat - 1
    has_prev, has_next = frame > 0, frame < nframe - 1

    cols = pl.ds(pl.multiple_of(c * HALF, HALF), HALF)
    x_copies = [pltpu.make_async_copy(x_ref.at[r], xs.at[0, 1 + r, c], x_sem.at[r]) for r in range(2)]
    w_copies = [
        pltpu.make_async_copy(wv_ref.at[:, cols], wv, w_sem.at[0]),
        pltpu.make_async_copy(wk_ref.at[:, cols], wk, w_sem.at[1]),
        pltpu.make_async_copy(wq_ref.at[:, cols], wq, w_sem.at[2]),
        pltpu.make_async_copy(wo_ref, wo, w_sem.at[3]),
    ]
    c_copies = [
        pltpu.make_async_copy(codes_hbm, codes_ref, c_sem.at[0]),
        pltpu.make_async_copy(counts_hbm, counts_ref, c_sem.at[1]),
    ]

    def remote(src, dst, ss, rs, dev):
        return pltpu.make_async_remote_copy(
            src_ref=src, dst_ref=dst, send_sem=ss, recv_sem=rs, device_id=dev, device_id_type=MESH
        )

    def part(i, size):
        start = BIG * i if size == BIG else 2 * BIG + SMALL * (i - 2)
        return pl.ds(pl.multiple_of(start, 16), size)

    def pieces():
        return [(i, BIG if i < 2 else SMALL) for i in range(NC)]

    def own_to_peer(r, lon):
        return remote(x_ref.at[r], xs.at[0, 1 + r, lon], p_ss.at[r], p_rs.at[r], {"lon": o})

    def to_next(r, i, size):
        k = r * NC + i
        return remote(x_ref.at[r, part(i, size)], xs.at[1, 1 + r, c, part(i, size)], y_ss.at[k], y_rs.at[k], {"frame": frame + 1})

    def side_dev(side):
        return {"lat": lat - 1 + 2 * side}

    def own_to_side(side, i, size):
        k = side * NC + i
        return remote(
            x_ref.at[side, part(i, size)], xs.at[0, 3 - 3 * side, c, part(i, size)], n0_ss.at[k], n0_rs.at[k], side_dev(side)
        )

    def prev_to_side(side, i, size):
        k = side * NC + i
        return remote(
            xs.at[1, 1 + side, c, part(i, size)], xs.at[1, 3 - 3 * side, c, part(i, size)], n1_ss.at[k], n1_rs.at[k], side_dev(side)
        )

    def forward(fr, row, i, size, lon):
        k = (fr * 4 + row) * NC + i
        block = xs.at[fr, row, lon, part(i, size)]
        return remote(block, block, f_ss.at[k], f_rs.at[k], {"lon": o})

    def bias_to_peer(lon):
        return remote(bias.at[lon], bias.at[lon], b_ss.at[0], b_rs.at[0], {"lon": o})

    def att_to_peer(r, lon):
        return remote(snd.at[r], full.at[r, lon], a_ss.at[r], a_rs.at[r], {"lon": o})

    send_to = (has_n, has_s)
    gets_from = (has_s, has_n)
    ra = jnp.where(lat % 4 == 3, 1, 0)
    rb = 1 - ra

    if COMM:
        barrier = pltpu.get_barrier_semaphore()

        def greet(dev):
            pl.semaphore_signal(barrier, inc=1, device_id=dev, device_id_type=MESH)

        greet({"lon": o})
        pl.when(has_n)(lambda: greet({"lat": lat - 1}))
        pl.when(has_s)(lambda: greet({"lat": lat + 1}))
        pl.when(has_prev)(lambda: greet({"frame": frame - 1}))
        pl.when(has_next)(lambda: greet({"frame": frame + 1}))

    for copy in x_copies + c_copies + w_copies:
        copy.start()

    if COMM:
        greeted = (
            1
            + has_n.astype(jnp.int32)
            + has_s.astype(jnp.int32)
            + has_prev.astype(jnp.int32)
            + has_next.astype(jnp.int32)
        )
        pl.semaphore_wait(barrier, greeted)
        for r in range(2):
            own_to_peer(r, c).start()

        @pl.when(has_next)
        def _():
            for i, size in pieces():
                to_next(ra, i, size).start()

        for side in range(2):

            @pl.when(send_to[side])
            def _(side=side):
                for i, size in pieces():
                    own_to_side(side, i, size).start()

        @pl.when(has_next)
        def _():
            for i, size in pieces():
                to_next(rb, i, size).start()

    ri = lax.broadcasted_iota(jnp.int32, (8, TOK), 0)
    li = lax.broadcasted_iota(jnp.int32, (8, TOK), 1)
    second = (li // TILE) % 2 == 1
    gcol = 2 * c + (li // TILE) % 2
    wcol = (ri - gcol + 5) % 4
    for copy in c_copies:
        copy.wait()
    outer = [jnp.where(has_n, 0, 3), jnp.where(has_s, 3, 0)]
    for r in range(2):
        first = jnp.minimum(jnp.maximum(2 * lat + r - 1, 0), 2 * nlat - 3) - 2 * lat + 1
        cnt = jnp.where(second, counts_ref[0, r, 1], counts_ref[0, r, 0])
        for slot in range(3):
            ext = outer[r] if slot == 0 else slot
            want = jnp.where(jnp.logical_and(wcol < 3, ri < 4), 3 * (ext - first) + wcol, -1)
            live = jnp.zeros((8, TOK), f32)
            for j in range(WIN):
                code = jnp.where(second, codes_ref[0, r, 1, j], codes_ref[0, r, 0, j])
                hit = jnp.logical_and(code == want, j < cnt)
                live = jnp.where(hit, 1.0, live)
            bias[c, r, slot] = jnp.where(live > 0.5, 0.0, DEAD)
    if COMM:
        bias_to_peer(c).start()
    vt[:, :, :, :, HEAD:, :] = jnp.ones((2, 4, 2, 8, VROWS - HEAD, TOK), bf16)
    w_copies[0].wait()
    wvt[...] = wv[...].T

    def pump_own_sides(i, size):
        if not COMM:
            return
        for side in range(2):

            @pl.when(gets_from[side])
            def _(side=side):
                own_to_side(side, i, size).wait_recv()
                forward(0, 3 - 3 * side, i, size, c).start()

    def pump_prev(r, i, size):
        if not COMM:
            return

        @pl.when(has_prev)
        def _():
            to_next(r, i, size).wait_recv()

            @pl.when(jnp.where(r == 0, has_n, has_s))
            def _():
                prev_to_side(r, i, size).start()

            forward(1, 1 + r, i, size, c).start()

    def pump_prev_side(side, i, size):
        if not COMM:
            return

        @pl.when(gets_from[side])
        def _():
            prev_to_side(side, i, size).wait_recv()
            forward(1, 3 - 3 * side, i, size, c).start()

    def await_forward(fr, row):
        if COMM:
            for i, size in pieces():
                forward(fr, row, i, size, o).wait_recv()

    def project(fr, pieces):
        x = jnp.concatenate([xs[fr, row, lon] for row, lon in pieces], axis=0)
        key = jnp.dot(x, wk[...], preferred_element_type=f32).astype(bf16)
        value = lax.dot_general(wvt[...], x, NT, preferred_element_type=f32).astype(bf16)
        for u, (row, lon) in enumerate(pieces):
            for pair in range(4):
                ks[fr, row, lon, pair] = key[u * TOK : (u + 1) * TOK, pair * 128 : (pair + 1) * 128]
            vt[fr, row, lon, :, :HEAD, :] = value[:, u * TOK : (u + 1) * TOK].reshape(8, HEAD, TOK)
        return x

    def attend(blocks, r, first, group, ahead):
        n = len(blocks)
        masks = []
        for _, _, slot in blocks:
            rows = jnp.concatenate([bias[0, r, slot], bias[1, r, slot]], axis=1)
            masks.append([rows[2 * u : 2 * u + 2].reshape(2, 1, 2 * TOK) for u in range(2)])

        def scores(h):
            best = None
            for k, (fr, row, _) in enumerate(blocks):
                key = jnp.concatenate([ks[fr, row, 0, h // 2], ks[fr, row, 1, h // 2]], axis=0)
                s = lax.dot_general(key, qz[r, h], NT, preferred_element_type=f32)
                ss[(h * n + k) % 8][...] = s
                s = s.reshape(2, TILE, 2, TILE, 2 * TOK)
                for u in range(2):
                    top = jnp.max(jnp.max(s[u], axis=0) + masks[k][u], axis=0)
                    best = top if best is None else jnp.maximum(best, top)
            m = jnp.maximum(jnp.max(best, axis=0, keepdims=True), FLOOR)
            if first:
                return m, None
            m_old = ms[r, h, :1]
            return jnp.maximum(m, m_old), m_old

        def values(h, m, m_old):
            total = None
            for k, (fr, row, _) in enumerate(blocks):
                s = ss[(h * n + k) % 8][...].reshape(2, TILE, 2, TILE, 2 * TOK)
                p = [jnp.exp(s[u] + (masks[k][u] - m)[None]).reshape(TOK, 2 * TOK).astype(bf16) for u in range(2)]
                value = jnp.concatenate([vt[fr, row, 0, h], vt[fr, row, 1, h]], axis=1)
                t = jnp.dot(value, jnp.concatenate(p, axis=0), preferred_element_type=f32)
                total = t if total is None else total + t
            if not first:
                total = total + os_[r, h] * jnp.exp(m_old - m)
            os_[r, h] = total
            ms[r, h] = jnp.broadcast_to(m, (8, 2 * TOK))

        steps = 8 // group
        state = {}
        for g in range(steps + ahead):
            if g < steps:
                for h in range(g * group, (g + 1) * group):
                    state[h] = scores(h)
            if g >= ahead:
                for h in range((g - ahead) * group, (g - ahead + 1) * group):
                    values(h, *state.pop(h))

    low = lax.broadcasted_iota(jnp.int32, (TOK, 128), 1) < HEAD
    for copy in x_copies:
        copy.wait()
    w_copies[1].wait()
    w_copies[2].wait()

    @pl.loop(0, 2)
    def _(t):
        lon = jnp.where(t == 0, c, o)

        @pl.when(t == 1)
        def _():
            if COMM:
                for r in range(2):
                    own_to_peer(r, o).wait_recv()
                bias_to_peer(o).wait_recv()

        x = project(0, [(1, lon), (2, lon)])
        query = jnp.dot(x, wq[...], preferred_element_type=f32).astype(bf16).astype(f32) * 0.125
        place = pl.ds(pl.multiple_of(lon * TOK, TOK), TOK)
        for r in range(2):
            for pair in range(4):
                q = query[r * TOK : (r + 1) * TOK, pair * 128 : (pair + 1) * 128]
                qz[r, 2 * pair, place] = jnp.where(low, q, 0.0).astype(bf16)
                qz[r, 2 * pair + 1, place] = jnp.where(low, 0.0, q).astype(bf16)

    @pl.loop(0, 2)
    def _(r):
        pump_prev(ra, r, BIG)
        pump_own_sides(r, BIG)
        attend([(0, 1, 1), (0, 2, 2)], r, True, 2, 1)

    for i in range(2, 4):
        pump_prev(ra, i, SMALL)
        pump_own_sides(i, SMALL)

    project(0, [(0, c), (3, c)])
    pump_prev(rb, 0, BIG)

    @pl.when(has_prev)
    def _():
        await_forward(1, 1 + ra)
        project(1, [(1 + ra, 0), (1 + ra, 1)])
        pump_prev(rb, 1, BIG)

    for side in range(2):
        pl.when(gets_from[side])(functools.partial(await_forward, 0, 3 - 3 * side))
    project(0, [(0, o), (3, o)])

    def outer_of(r):
        return jnp.where(r == 0, outer[0], outer[1])

    @pl.loop(0, 2)
    def _(r):
        pump_prev(rb, 2 + r, SMALL)

        @pl.when(has_prev)
        def _():
            attend([(0, outer_of(r), 0), (1, 1 + ra, 1 + ra)], r, False, 2, 1)

        @pl.when(jnp.logical_not(has_prev))
        def _():
            attend([(0, outer_of(r), 0)], r, False, 4, 1)

    both_sides = jnp.logical_and(has_n, has_s)

    @pl.when(has_prev)
    def _():
        await_forward(1, 1 + rb)
        project(1, [(1 + rb, 0), (1 + rb, 1)])
        for side in range(2):
            for i in range(2):
                pump_prev_side(side, i, BIG)
        @pl.loop(0, 2)
        def _(r):
            attend([(1, 1 + rb, 1 + rb)], r, False, 4, 1)

        for i in range(2, 4):
            for side in range(2):
                pump_prev_side(side, i, SMALL)

        project(1, [(0, c), (3, c)])
        for side in range(2):
            pl.when(gets_from[side])(functools.partial(await_forward, 1, 3 - 3 * side))
        project(1, [(0, o), (3, o)])
        attend([(1, outer[1], 0)], 1, False, 4, 1)

    mine_first = c == 0

    def finish(r):
        for h in range(8):
            total = os_[r, h]
            att = (total[:HEAD] * (1.0 / total[HEAD : HEAD + 1])).astype(bf16)
            rows = pl.ds(h * HEAD, HEAD)
            full[r, c, rows] = jnp.where(mine_first, att[:, :TOK], att[:, TOK:])
            snd[r, rows] = jnp.where(mine_first, att[:, TOK:], att[:, :TOK])
        if COMM:
            att_to_peer(r, c).start()

    def half_out(r, half):
        rows = pl.ds(pl.multiple_of(half * HALF, HALF), HALF)
        return lax.dot_general(full[r, half], wo[rows, :], TN, preferred_element_type=f32)

    def put_out(r):
        if COMM:
            att_to_peer(r, o).wait_recv()
        out_ref[r] = (part_out[r] + half_out(r, o)).astype(bf16)

    finish(1)

    @pl.when(has_prev)
    def _():
        attend([(1, outer[0], 0)], 0, False, 4, 1)

    finish(0)
    w_copies[3].wait()

    @pl.loop(0, 2)
    def _(r):
        part_out[r] = half_out(r, c)

    @pl.loop(0, 2)
    def _(t):
        put_out(1 - t)

    if COMM:
        for r in range(2):
            own_to_peer(r, c).wait_send()
            att_to_peer(r, c).wait_send()
        bias_to_peer(c).wait_send()

        @pl.when(has_next)
        def _():
            for r in range(2):
                for i, size in pieces():
                    to_next(r, i, size).wait_send()

        for side in range(2):

            @pl.when(send_to[side])
            def _(side=side):
                for i, size in pieces():
                    own_to_side(side, i, size).wait_send()

            @pl.when(gets_from[side])
            def _(side=side):
                for i, size in pieces():
                    forward(0, 3 - 3 * side, i, size, c).wait_send()

        @pl.when(has_prev)
        def _():
            for side in range(2):
                for i, size in pieces():
                    forward(1, 1 + side, i, size, c).wait_send()

                @pl.when(send_to[side])
                def _(side=side):
                    for i, size in pieces():
                        prev_to_side(side, i, size).wait_send()

                @pl.when(gets_from[side])
                def _(side=side):
                    for i, size in pieces():
                        forward(1, 3 - 3 * side, i, size, c).wait_send()


def on_device(frames_in, w_query, w_key, w_value, w_out, codes, counts):
    shape = frames_in.shape
    x = frames_in.reshape(2, TOK, D)
    bf16, f32 = jnp.bfloat16, jnp.float32
    dma = pltpu.SemaphoreType.DMA
    out = pl.pallas_call(
        kernel,
        out_shape=jax.ShapeDtypeStruct((2, TOK, D), bf16),
        in_specs=[pl.BlockSpec(memory_space=pltpu.HBM)] * 7,
        out_specs=pl.BlockSpec(memory_space=pltpu.VMEM),
        scratch_shapes=[
            pltpu.SMEM((1, 2, 2, WIN), jnp.int32),
            pltpu.SMEM((1, 2, 2), jnp.int32),
            pltpu.VMEM((2, 4, 2, TOK, D), bf16),
            pltpu.VMEM((D, HALF), bf16),
            pltpu.VMEM((D, HALF), bf16),
            pltpu.VMEM((D, HALF), bf16),
            pltpu.VMEM((D, D), bf16),
            pltpu.VMEM((HALF, D), bf16),
            pltpu.VMEM((2, 8, 2 * TOK, 128), bf16),
            pltpu.VMEM((2, 4, 2, 4, TOK, 128), bf16),
            pltpu.VMEM((2, 4, 2, 8, VROWS, TOK), bf16),
            pltpu.VMEM((2, 8, VROWS, 2 * TOK), f32),
            pltpu.VMEM((2, 8, 8, 2 * TOK), f32),
            pltpu.VMEM((2, 2, 3, 8, TOK), f32),
            pltpu.VMEM((2, HALF, TOK), bf16),
            pltpu.VMEM((2, 2, HALF, TOK), bf16),
            pltpu.VMEM((2, TOK, D), f32),
            *([pltpu.VMEM((2 * TOK, 2 * TOK), f32)] * 8),
            dma((4,)),
            dma((2,)),
            dma((2,)),
            dma((2,)),
            dma((2,)),
            dma((2 * NC,)),
            dma((2 * NC,)),
            dma((2 * NC,)),
            dma((2 * NC,)),
            dma((2 * NC,)),
            dma((2 * NC,)),
            dma((8 * NC,)),
            dma((8 * NC,)),
            dma((1,)),
            dma((1,)),
            dma((2,)),
            dma((2,)),
        ],
        compiler_params=pltpu.CompilerParams(
            vmem_limit_bytes=44 << 20,
            **(dict(collective_id=0, has_side_effects=True) if COMM else {}),
        ),
        cost_estimate=pl.CostEstimate(flops=12 * 10**9, bytes_accessed=8 << 20, transcendentals=6 << 20),
    )(*[pltpu.with_memory_space_constraint(v, pltpu.HBM) for v in (x, w_query, w_key, w_value, w_out, codes, counts)])
    return out.reshape(shape)


def solution(mesh):
    placed = (
        P("frame", "lat", "lon", None),
        P(),
        P(),
        P(),
        P(),
        P("frame", "lat", "lon", None),
        P("frame", "lat", "lon"),
    )
    return jax.shard_map(
        on_device,
        mesh=mesh,
        in_specs=placed,
        out_specs=P("frame", "lat", "lon", None),
        check_vma=False,
    )
```

```python
import functools

import jax
import jax.numpy as jnp
from jax import lax
from jax.experimental import pallas as pl
from jax.experimental.pallas import tpu as pltpu
from jax.sharding import PartitionSpec as P

HEADS = 16
HEAD = 64
TILE = 8
WIN = 9
D = 1024
HALF = D // 2
TOK = 128
NC = 4
BIG, SMALL = 32, 32
VROWS = HEAD + 16
DEAD = -1e38
FLOOR = -1e30
MESH = pl.DeviceIdType.MESH
COMM = True
NT = (((1,), (1,)), ((), ()))
TN = (((0,), (0,)), ((), ()))


def kernel(
    x_ref, wq_ref, wk_ref, wv_ref, wo_ref, codes_hbm, counts_hbm, out_ref,
    codes_ref, counts_ref, xs, wq, wk, wv, wo, wvt, qz, ks, vt, os_, ms, bias, snd, full, part_out,
    s0, s1, s2, s3, s4, s5, s6, s7,
    w_sem, x_sem, c_sem,
    p_ss, p_rs, y_ss, y_rs, n0_ss, n0_rs, n1_ss, n1_rs, f_ss, f_rs, b_ss, b_rs, a_ss, a_rs,
):
    f32, bf16 = jnp.float32, jnp.bfloat16
    lat, c, frame = lax.axis_index("lat"), lax.axis_index("lon"), lax.axis_index("frame")
    nlat, nframe = lax.axis_size("lat"), lax.axis_size("frame")
    o = 1 - c
    ss = (s0, s1, s2, s3, s4, s5, s6, s7)
    has_n, has_s = lat > 0, lat < nlat - 1
    has_prev, has_next = frame > 0, frame < nframe - 1

    cols = pl.ds(pl.multiple_of(c * HALF, HALF), HALF)
    x_copies = [pltpu.make_async_copy(x_ref.at[r], xs.at[0, 1 + r, c], x_sem.at[r]) for r in range(2)]
    w_copies = [
        pltpu.make_async_copy(wv_ref.at[:, cols], wv, w_sem.at[0]),
        pltpu.make_async_copy(wk_ref.at[:, cols], wk, w_sem.at[1]),
        pltpu.make_async_copy(wq_ref.at[:, cols], wq, w_sem.at[2]),
        pltpu.make_async_copy(wo_ref, wo, w_sem.at[3]),
    ]
    c_copies = [
        pltpu.make_async_copy(codes_hbm, codes_ref, c_sem.at[0]),
        pltpu.make_async_copy(counts_hbm, counts_ref, c_sem.at[1]),
    ]

    def remote(src, dst, ss, rs, dev):
        return pltpu.make_async_remote_copy(
            src_ref=src, dst_ref=dst, send_sem=ss, recv_sem=rs, device_id=dev, device_id_type=MESH
        )

    def part(i, size):
        start = BIG * i if size == BIG else 2 * BIG + SMALL * (i - 2)
        return pl.ds(pl.multiple_of(start, 16), size)

    def pieces():
        return [(i, BIG if i < 2 else SMALL) for i in range(NC)]

    def own_to_peer(r, lon):
        return remote(x_ref.at[r], xs.at[0, 1 + r, lon], p_ss.at[r], p_rs.at[r], {"lon": o})

    def to_next(r, i, size):
        k = r * NC + i
        return remote(x_ref.at[r, part(i, size)], xs.at[1, 1 + r, c, part(i, size)], y_ss.at[k], y_rs.at[k], {"frame": frame + 1})

    def side_dev(side):
        return {"lat": lat - 1 + 2 * side}

    def own_to_side(side, i, size):
        k = side * NC + i
        return remote(
            x_ref.at[side, part(i, size)], xs.at[0, 3 - 3 * side, c, part(i, size)], n0_ss.at[k], n0_rs.at[k], side_dev(side)
        )

    def prev_to_side(side, i, size):
        k = side * NC + i
        return remote(
            xs.at[1, 1 + side, c, part(i, size)], xs.at[1, 3 - 3 * side, c, part(i, size)], n1_ss.at[k], n1_rs.at[k], side_dev(side)
        )

    def forward(fr, row, i, size, lon):
        k = (fr * 4 + row) * NC + i
        block = xs.at[fr, row, lon, part(i, size)]
        return remote(block, block, f_ss.at[k], f_rs.at[k], {"lon": o})

    def bias_to_peer(lon):
        return remote(bias.at[lon], bias.at[lon], b_ss.at[0], b_rs.at[0], {"lon": o})

    def att_to_peer(r, lon):
        return remote(snd.at[r], full.at[r, lon], a_ss.at[r], a_rs.at[r], {"lon": o})

    send_to = (has_n, has_s)
    gets_from = (has_s, has_n)
    ra = jnp.where(lat % 4 == 3, 1, 0)
    rb = 1 - ra

    if COMM:
        barrier = pltpu.get_barrier_semaphore()

        def greet(dev):
            pl.semaphore_signal(barrier, inc=1, device_id=dev, device_id_type=MESH)

        greet({"lon": o})
        pl.when(has_n)(lambda: greet({"lat": lat - 1}))
        pl.when(has_s)(lambda: greet({"lat": lat + 1}))
        pl.when(has_prev)(lambda: greet({"frame": frame - 1}))
        pl.when(has_next)(lambda: greet({"frame": frame + 1}))

    for copy in x_copies + c_copies + w_copies:
        copy.start()

    if COMM:
        greeted = (
            1
            + has_n.astype(jnp.int32)
            + has_s.astype(jnp.int32)
            + has_prev.astype(jnp.int32)
            + has_next.astype(jnp.int32)
        )
        pl.semaphore_wait(barrier, greeted)
        for r in range(2):
            own_to_peer(r, c).start()

        @pl.when(has_next)
        def _():
            for i, size in pieces():
                to_next(ra, i, size).start()

        for side in range(2):

            @pl.when(send_to[side])
            def _(side=side):
                for i, size in pieces():
                    own_to_side(side, i, size).start()

        @pl.when(has_next)
        def _():
            for i, size in pieces():
                to_next(rb, i, size).start()

    ri = lax.broadcasted_iota(jnp.int32, (8, TOK), 0)
    li = lax.broadcasted_iota(jnp.int32, (8, TOK), 1)
    second = (li // TILE) % 2 == 1
    gcol = 2 * c + (li // TILE) % 2
    wcol = (ri - gcol + 5) % 4
    for copy in c_copies:
        copy.wait()
    outer = [jnp.where(has_n, 0, 3), jnp.where(has_s, 3, 0)]
    for r in range(2):
        first = jnp.minimum(jnp.maximum(2 * lat + r - 1, 0), 2 * nlat - 3) - 2 * lat + 1
        cnt = jnp.where(second, counts_ref[0, r, 1], counts_ref[0, r, 0])
        for slot in range(3):
            ext = outer[r] if slot == 0 else slot
            want = jnp.where(jnp.logical_and(wcol < 3, ri < 4), 3 * (ext - first) + wcol, -1)
            live = jnp.zeros((8, TOK), f32)
            for j in range(WIN):
                code = jnp.where(second, codes_ref[0, r, 1, j], codes_ref[0, r, 0, j])
                hit = jnp.logical_and(code == want, j < cnt)
                live = jnp.where(hit, 1.0, live)
            bias[c, r, slot] = jnp.where(live > 0.5, 0.0, DEAD)
    if COMM:
        bias_to_peer(c).start()
    vt[:, :, :, :, HEAD:, :] = jnp.ones((2, 4, 2, 8, VROWS - HEAD, TOK), bf16)
    w_copies[0].wait()
    wvt[...] = wv[...].T

    def pump_own_sides(i, size):
        if not COMM:
            return
        for side in range(2):

            @pl.when(gets_from[side])
            def _(side=side):
                own_to_side(side, i, size).wait_recv()
                forward(0, 3 - 3 * side, i, size, c).start()

    def pump_prev(r, i, size):
        if not COMM:
            return

        @pl.when(has_prev)
        def _():
            to_next(r, i, size).wait_recv()

            @pl.when(jnp.where(r == 0, has_n, has_s))
            def _():
                prev_to_side(r, i, size).start()

            forward(1, 1 + r, i, size, c).start()

    def pump_prev_side(side, i, size):
        if not COMM:
            return

        @pl.when(gets_from[side])
        def _():
            prev_to_side(side, i, size).wait_recv()
            forward(1, 3 - 3 * side, i, size, c).start()

    def await_forward(fr, row):
        if COMM:
            for i, size in pieces():
                forward(fr, row, i, size, o).wait_recv()

    def project(fr, pieces):
        x = jnp.concatenate([xs[fr, row, lon] for row, lon in pieces], axis=0)
        key = jnp.dot(x, wk[...], preferred_element_type=f32).astype(bf16)
        value = lax.dot_general(wvt[...], x, NT, preferred_element_type=f32).astype(bf16)
        for u, (row, lon) in enumerate(pieces):
            for pair in range(4):
                ks[fr, row, lon, pair] = key[u * TOK : (u + 1) * TOK, pair * 128 : (pair + 1) * 128]
            vt[fr, row, lon, :, :HEAD, :] = value[:, u * TOK : (u + 1) * TOK].reshape(8, HEAD, TOK)
        return x

    def attend(blocks, r, first, group, ahead):
        n = len(blocks)
        masks = []
        for _, _, slot in blocks:
            rows = jnp.concatenate([bias[0, r, slot], bias[1, r, slot]], axis=1)
            masks.append([rows[2 * u : 2 * u + 2].reshape(2, 1, 2 * TOK) for u in range(2)])

        def scores(h):
            best = None
            for k, (fr, row, _) in enumerate(blocks):
                key = jnp.concatenate([ks[fr, row, 0, h // 2], ks[fr, row, 1, h // 2]], axis=0)
                s = lax.dot_general(key, qz[r, h], NT, preferred_element_type=f32)
                ss[(h * n + k) % 8][...] = s
                s = s.reshape(2, TILE, 2, TILE, 2 * TOK)
                for u in range(2):
                    top = jnp.max(jnp.max(s[u], axis=0) + masks[k][u], axis=0)
                    best = top if best is None else jnp.maximum(best, top)
            m = jnp.maximum(jnp.max(best, axis=0, keepdims=True), FLOOR)
            if first:
                return m, None
            m_old = ms[r, h, :1]
            return jnp.maximum(m, m_old), m_old

        def values(h, m, m_old):
            total = None
            for k, (fr, row, _) in enumerate(blocks):
                s = ss[(h * n + k) % 8][...].reshape(2, TILE, 2, TILE, 2 * TOK)
                p = [jnp.exp(s[u] + (masks[k][u] - m)[None]).reshape(TOK, 2 * TOK).astype(bf16) for u in range(2)]
                value = jnp.concatenate([vt[fr, row, 0, h], vt[fr, row, 1, h]], axis=1)
                t = jnp.dot(value, jnp.concatenate(p, axis=0), preferred_element_type=f32)
                total = t if total is None else total + t
            if not first:
                total = total + os_[r, h] * jnp.exp(m_old - m)
            os_[r, h] = total
            ms[r, h] = jnp.broadcast_to(m, (8, 2 * TOK))

        steps = 8 // group
        state = {}
        for g in range(steps + ahead):
            if g < steps:
                for h in range(g * group, (g + 1) * group):
                    state[h] = scores(h)
            if g >= ahead:
                for h in range((g - ahead) * group, (g - ahead + 1) * group):
                    values(h, *state.pop(h))

    low = lax.broadcasted_iota(jnp.int32, (TOK, 128), 1) < HEAD
    for copy in x_copies:
        copy.wait()
    w_copies[1].wait()
    w_copies[2].wait()

    @pl.loop(0, 2)
    def _(t):
        lon = jnp.where(t == 0, c, o)

        @pl.when(t == 1)
        def _():
            if COMM:
                for r in range(2):
                    own_to_peer(r, o).wait_recv()
                bias_to_peer(o).wait_recv()

        x = project(0, [(1, lon), (2, lon)])
        query = jnp.dot(x, wq[...], preferred_element_type=f32).astype(bf16).astype(f32) * 0.125
        place = pl.ds(pl.multiple_of(lon * TOK, TOK), TOK)
        for r in range(2):
            for pair in range(4):
                q = query[r * TOK : (r + 1) * TOK, pair * 128 : (pair + 1) * 128]
                qz[r, 2 * pair, place] = jnp.where(low, q, 0.0).astype(bf16)
                qz[r, 2 * pair + 1, place] = jnp.where(low, 0.0, q).astype(bf16)

    @pl.loop(0, 2)
    def _(r):
        pump_own_sides(r, BIG)
        pump_prev(ra, r, BIG)
        attend([(0, 1, 1), (0, 2, 2)], r, True, 2, 1)

    for i in range(2, 4):
        pump_prev(ra, i, SMALL)
        pump_own_sides(i, SMALL)

    project(0, [(0, c), (3, c)])
    pump_prev(rb, 0, BIG)

    @pl.when(has_prev)
    def _():
        await_forward(1, 1 + ra)
        project(1, [(1 + ra, 0), (1 + ra, 1)])
        pump_prev(rb, 1, BIG)

    for side in range(2):
        pl.when(gets_from[side])(functools.partial(await_forward, 0, 3 - 3 * side))
    project(0, [(0, o), (3, o)])

    def outer_of(r):
        return jnp.where(r == 0, outer[0], outer[1])

    @pl.loop(0, 2)
    def _(r):
        pump_prev(rb, 2 + r, SMALL)

        @pl.when(has_prev)
        def _():
            attend([(0, outer_of(r), 0), (1, 1 + ra, 1 + ra)], r, False, 2, 1)

        @pl.when(jnp.logical_not(has_prev))
        def _():
            attend([(0, outer_of(r), 0)], r, False, 4, 1)

    both_sides = jnp.logical_and(has_n, has_s)

    @pl.when(has_prev)
    def _():
        await_forward(1, 1 + rb)
        project(1, [(1 + rb, 0), (1 + rb, 1)])
        for side in range(2):
            for i in range(2):
                pump_prev_side(side, i, BIG)
        @pl.loop(0, 2)
        def _(r):
            attend([(1, 1 + rb, 1 + rb)], r, False, 4, 1)

        for i in range(2, 4):
            for side in range(2):
                pump_prev_side(side, i, SMALL)

        project(1, [(0, c), (3, c)])
        for side in range(2):
            pl.when(gets_from[side])(functools.partial(await_forward, 1, 3 - 3 * side))
        project(1, [(0, o), (3, o)])
        attend([(1, outer[1], 0)], 1, False, 4, 1)

    mine_first = c == 0

    def finish(r):
        for h in range(8):
            total = os_[r, h]
            att = (total[:HEAD] * (1.0 / total[HEAD : HEAD + 1])).astype(bf16)
            rows = pl.ds(h * HEAD, HEAD)
            full[r, c, rows] = jnp.where(mine_first, att[:, :TOK], att[:, TOK:])
            snd[r, rows] = jnp.where(mine_first, att[:, TOK:], att[:, :TOK])
        if COMM:
            att_to_peer(r, c).start()

    def half_out(r, half):
        rows = pl.ds(pl.multiple_of(half * HALF, HALF), HALF)
        return lax.dot_general(full[r, half], wo[rows, :], TN, preferred_element_type=f32)

    def put_out(r):
        if COMM:
            att_to_peer(r, o).wait_recv()
        out_ref[r] = (part_out[r] + half_out(r, o)).astype(bf16)

    finish(1)

    @pl.when(has_prev)
    def _():
        attend([(1, outer[0], 0)], 0, False, 4, 1)

    finish(0)
    w_copies[3].wait()

    @pl.loop(0, 2)
    def _(r):
        part_out[r] = half_out(r, c)

    @pl.loop(0, 2)
    def _(t):
        put_out(1 - t)

    if COMM:
        for r in range(2):
            own_to_peer(r, c).wait_send()
            att_to_peer(r, c).wait_send()
        bias_to_peer(c).wait_send()

        @pl.when(has_next)
        def _():
            for r in range(2):
                for i, size in pieces():
                    to_next(r, i, size).wait_send()

        for side in range(2):

            @pl.when(send_to[side])
            def _(side=side):
                for i, size in pieces():
                    own_to_side(side, i, size).wait_send()

            @pl.when(gets_from[side])
            def _(side=side):
                for i, size in pieces():
                    forward(0, 3 - 3 * side, i, size, c).wait_send()

        @pl.when(has_prev)
        def _():
            for side in range(2):
                for i, size in pieces():
                    forward(1, 1 + side, i, size, c).wait_send()

                @pl.when(send_to[side])
                def _(side=side):
                    for i, size in pieces():
                        prev_to_side(side, i, size).wait_send()

                @pl.when(gets_from[side])
                def _(side=side):
                    for i, size in pieces():
                        forward(1, 3 - 3 * side, i, size, c).wait_send()


def on_device(frames_in, w_query, w_key, w_value, w_out, codes, counts):
    shape = frames_in.shape
    x = frames_in.reshape(2, TOK, D)
    bf16, f32 = jnp.bfloat16, jnp.float32
    dma = pltpu.SemaphoreType.DMA
    out = pl.pallas_call(
        kernel,
        out_shape=jax.ShapeDtypeStruct((2, TOK, D), bf16),
        in_specs=[pl.BlockSpec(memory_space=pltpu.HBM)] * 7,
        out_specs=pl.BlockSpec(memory_space=pltpu.VMEM),
        scratch_shapes=[
            pltpu.SMEM((1, 2, 2, WIN), jnp.int32),
            pltpu.SMEM((1, 2, 2), jnp.int32),
            pltpu.VMEM((2, 4, 2, TOK, D), bf16),
            pltpu.VMEM((D, HALF), bf16),
            pltpu.VMEM((D, HALF), bf16),
            pltpu.VMEM((D, HALF), bf16),
            pltpu.VMEM((D, D), bf16),
            pltpu.VMEM((HALF, D), bf16),
            pltpu.VMEM((2, 8, 2 * TOK, 128), bf16),
            pltpu.VMEM((2, 4, 2, 4, TOK, 128), bf16),
            pltpu.VMEM((2, 4, 2, 8, VROWS, TOK), bf16),
            pltpu.VMEM((2, 8, VROWS, 2 * TOK), f32),
            pltpu.VMEM((2, 8, 8, 2 * TOK), f32),
            pltpu.VMEM((2, 2, 3, 8, TOK), f32),
            pltpu.VMEM((2, HALF, TOK), bf16),
            pltpu.VMEM((2, 2, HALF, TOK), bf16),
            pltpu.VMEM((2, TOK, D), f32),
            *([pltpu.VMEM((2 * TOK, 2 * TOK), f32)] * 8),
            dma((4,)),
            dma((2,)),
            dma((2,)),
            dma((2,)),
            dma((2,)),
            dma((2 * NC,)),
            dma((2 * NC,)),
            dma((2 * NC,)),
            dma((2 * NC,)),
            dma((2 * NC,)),
            dma((2 * NC,)),
            dma((8 * NC,)),
            dma((8 * NC,)),
            dma((1,)),
            dma((1,)),
            dma((2,)),
            dma((2,)),
        ],
        compiler_params=pltpu.CompilerParams(
            vmem_limit_bytes=44 << 20,
            **(dict(collective_id=0, has_side_effects=True) if COMM else {}),
        ),
        cost_estimate=pl.CostEstimate(flops=12 * 10**9, bytes_accessed=8 << 20, transcendentals=6 << 20),
    )(*[pltpu.with_memory_space_constraint(v, pltpu.HBM) for v in (x, w_query, w_key, w_value, w_out, codes, counts)])
    return out.reshape(shape)


def solution(mesh):
    placed = (
        P("frame", "lat", "lon", None),
        P(),
        P(),
        P(),
        P(),
        P("frame", "lat", "lon", None),
        P("frame", "lat", "lon"),
    )
    return jax.shard_map(
        on_device,
        mesh=mesh,
        in_specs=placed,
        out_specs=P("frame", "lat", "lon", None),
        check_vma=False,
    )
```
